32 devices in a mesh: rows: 16 (over z, y, core), cols: 2 (over x).
Axes of the slice: x: 2, y: 2, z: 4, core: 2. Of those that a mesh axis runs over, the one named last changes fastest.
Arguments:
- pair: bfloat16 [384, 384, 128], P('rows', 'cols'), may hold values from -6 to 6
- token_mask: int32 [384], P('cols'), may hold values from 0 to 1
- norm_gain: float32 [128], replicated, may hold values from 0.25 to 1.75
- norm_shift: float32 [128], replicated, may hold values from -3 to 3
- in_weight: bfloat16 [128, 512], replicated, may hold values from -1.5 to 1.5
- gate_bias: float32 [128], replicated, may hold values from -4 to 4
- bias_weight: bfloat16 [128, 4], replicated, may hold values from -16 to 16
- out_weight: bfloat16 [128, 128], replicated, may hold values from -1.5 to 1.5
- out_bias: float32 [128], replicated, may hold values from -1.8 to 1.8
Outputs:
- updated: bfloat16 [384, 384, 128], P('rows', 'cols')
The draws below stay inside these ranges and needn't reach their ends.
All inputs are finite; a program needn't handle non-finite values.
Results may differ from the reference program's by a relative error of at most 0.006.
The reference program's roundings to bfloat16 on the way count: a program that leaves them out, or rounds other values in their place, can miss the bound.
Values may be sent and summed in bfloat16 or wider, within the bound.
No kernel may reach another device: no remote copies, remote signals or barrier semaphores. Data moves between devices by JAX's collectives and lax.ppermute only.
A program may use at most 128 MiB of HBM per device.

```python
import jax
import jax.numpy as jnp
from jax import lax

CHANNELS = 128
HEADS = 4
HEAD_DIM = 32
TOKENS = 384


def head_directions(key):
    return jax.random.normal(jax.random.fold_in(key, 11), (CHANNELS, HEADS), jnp.float32)


def channel_direction(key):
    return jax.random.normal(jax.random.fold_in(key, 31), (CHANNELS,), jnp.float32) / jnp.sqrt(jnp.float32(CHANNELS))


def head_coupling(key):
    signs = 2.0 * jax.random.randint(jax.random.fold_in(key, 32), (HEADS,), 0, 2).astype(jnp.float32) - 1.0
    sizes = jax.random.uniform(jax.random.fold_in(key, 33), (HEADS,), jnp.float32, 0.3, 0.5)
    return signs * sizes


def value_coupling(key):
    inner_width = HEADS * HEAD_DIM
    signs = 2.0 * jax.random.randint(jax.random.fold_in(key, 34), (inner_width,), 0, 2).astype(jnp.float32) - 1.0
    sizes = jax.random.uniform(jax.random.fold_in(key, 35), (inner_width,), jnp.float32, 0.7, 1.3)
    return signs * sizes


def draw_bias_weight(key, part):
    spread_part = head_directions(key) / jnp.sqrt(jnp.float32(CHANNELS))
    coupled = channel_direction(key)[:, None] * head_coupling(key)[None, :]
    base = 0.3 * spread_part + coupled
    return jnp.clip(base, -16.0, 16.0).astype(jnp.bfloat16)


def draw_in_weight(key, part):
    inner_width = HEADS * HEAD_DIM
    noise = jax.random.normal(jax.random.fold_in(key, 41), (CHANNELS, 4 * inner_width), jnp.float32)
    drawn = 1.0 / jnp.sqrt(jnp.float32(CHANNELS))
    front = drawn * jnp.ones((2 * inner_width,), jnp.float32)
    scales = jnp.concatenate((front, drawn * jnp.ones((2 * inner_width,), jnp.float32)))
    weight = noise * scales[None, :]
    coupling_row = jnp.concatenate((jnp.zeros((2 * inner_width,), jnp.float32), value_coupling(key), jnp.zeros((inner_width,), jnp.float32)))
    weight = weight + channel_direction(key)[:, None] * coupling_row[None, :]
    return jnp.clip(weight, -1.5, 1.5).astype(jnp.bfloat16)


def draw_pair(key, part):
    field = jax.random.normal(jax.random.fold_in(key, 5), (TOKENS, TOKENS, CHANNELS), jnp.float32)
    column_part = 1.5 * jax.random.normal(jax.random.fold_in(key, 36), (TOKENS,), jnp.float32)
    rough_part = 0.8 * jax.random.normal(jax.random.fold_in(key, 37), (TOKENS, TOKENS), jnp.float32)
    scalar_field = column_part[None, :] + rough_part
    field = field + scalar_field[:, :, None] * channel_direction(key)[None, None, :]
    return jnp.clip(field, -6.0, 6.0).astype(jnp.bfloat16)


def draw_token_mask(key, part):
    kept = (jax.random.randint(jax.random.fold_in(key, 23), (TOKENS,), 0, 32) != 0).astype(jnp.int32)
    anchor = jax.random.randint(jax.random.fold_in(key, 24), (), 0, TOKENS)
    missing = (anchor + jax.random.randint(jax.random.fold_in(key, 25), (), 1, TOKENS)) % TOKENS
    kept = kept.at[missing].set(0)
    return kept.at[anchor].set(1)


def scatter_about(own_key, extent, scale, limit, dtype=jnp.bfloat16):
    array = scale * jax.random.normal(own_key, extent, jnp.float32)
    return jnp.clip(array, min=-limit, max=limit).astype(dtype)


def setup_inputs(seed: int = 0) -> dict:
    key_list = jax.random.split(jax.random.key(seed), 10)
    pair = draw_pair(jax.random.fold_in(key_list[9], 71), 0)
    token_mask = draw_token_mask(jax.random.fold_in(key_list[9], 71), 0)
    norm_gain = jnp.clip(1.0 + 0.15 * jax.random.normal(key_list[2], (CHANNELS,), jnp.float32), 0.25, 1.75)
    norm_shift = scatter_about(key_list[3], (CHANNELS,), 0.5, 3.0, jnp.float32)
    in_weight = draw_in_weight(jax.random.fold_in(key_list[9], 71), 0)
    gate_bias = scatter_about(key_list[5], (HEADS * HEAD_DIM,), 1.0, 4.0, jnp.float32)
    bias_weight = draw_bias_weight(jax.random.fold_in(key_list[9], 71), 0)
    out_weight = scatter_about(key_list[7], (HEADS * HEAD_DIM, CHANNELS), 0.25, 1.5)
    out_bias = scatter_about(key_list[8], (CHANNELS,), 0.3, 1.8, jnp.float32)
    return {"pair": pair, "token_mask": token_mask, "norm_gain": norm_gain, "norm_shift": norm_shift, "in_weight": in_weight, "gate_bias": gate_bias, "bias_weight": bias_weight, "out_weight": out_weight, "out_bias": out_bias}


def layer_norm(pair_block, norm_gain, norm_shift):
    as_float = pair_block.astype(jnp.float32)
    center = lax.optimization_barrier(jnp.mean(as_float, axis=-1, keepdims=True))
    spread = lax.optimization_barrier(jnp.mean(jnp.square(as_float - center), axis=-1, keepdims=True))
    return ((as_float - center) * lax.rsqrt(spread + 1e-05) * norm_gain + norm_shift).astype(jnp.bfloat16)

def reference(pair, token_mask, norm_gain, norm_shift, in_weight, gate_bias, bias_weight, out_weight, out_bias):
    inner_width = HEADS * HEAD_DIM

    def bias_row(pair_row):
        normed = layer_norm(pair_row, norm_gain, norm_shift)
        return jnp.dot(normed, bias_weight, preferred_element_type=jnp.float32).astype(jnp.bfloat16)
    pair_bias = lax.map(bias_row, pair)
    bias_heads = jnp.transpose(pair_bias, (0, 2, 1)).astype(jnp.float32)
    masking = 1000000000.0 * (token_mask.astype(jnp.float32) - 1.0)

    def attend_row(pair_row):
        normed = layer_norm(pair_row, norm_gain, norm_shift)
        projected = jnp.dot(normed, in_weight, preferred_element_type=jnp.float32)
        queries = (projected[:, :inner_width] * HEAD_DIM ** (-0.5)).astype(jnp.bfloat16).reshape(TOKENS, HEADS, HEAD_DIM)
        keys_row = projected[:, inner_width:2 * inner_width].astype(jnp.bfloat16).reshape(TOKENS, HEADS, HEAD_DIM)
        values_row = projected[:, 2 * inner_width:3 * inner_width].astype(jnp.bfloat16).reshape(TOKENS, HEADS, HEAD_DIM)
        gates = jax.nn.sigmoid(projected[:, 3 * inner_width:] + gate_bias)
        scores = jnp.einsum('jhd,khd->jhk', queries.astype(jnp.float32), keys_row.astype(jnp.float32))
        scores = scores + bias_heads + masking
        top = lax.optimization_barrier(jnp.max(scores, axis=-1, keepdims=True))
        expo = jnp.exp(scores - top)
        totals = lax.optimization_barrier(jnp.sum(expo, axis=-1))
        weights = lax.optimization_barrier(expo.astype(jnp.bfloat16))
        summed = jnp.einsum('jhk,khd->jhd', weights.astype(jnp.float32), values_row.astype(jnp.float32))
        attended = summed / totals[..., None]
        gated = (gates * attended.reshape(TOKENS, inner_width)).astype(jnp.bfloat16)
        return (jnp.dot(gated, out_weight, preferred_element_type=jnp.float32) + out_bias).astype(jnp.bfloat16)
    return lax.map(attend_row, pair)
```

```python
import functools

import jax
import jax.numpy as jnp
import numpy as np
from jax import lax
from jax.experimental import pallas as pl
from jax.experimental.pallas import tpu as pltpu
from jax.sharding import PartitionSpec as P

LANES = 128
MISSING = -1e9
NN = (((1,), (0,)), ((), ()))
NT = (((1,), (1,)), ((), ()))
TN = (((0,), (0,)), ((), ()))
CHUNKS = 3


def dot(left, right, dims=NN):
    return lax.dot_general(left, right, dims, preferred_element_type=jnp.float32)


def layer_norm(pair_block, norm_gain, norm_shift):
    as_float = pair_block.astype(jnp.float32)
    center = jnp.mean(as_float, axis=-1, keepdims=True)
    spread = jnp.mean(jnp.square(as_float - center), axis=-1, keepdims=True)
    return ((as_float - center) * lax.rsqrt(spread + 1e-05) * norm_gain + norm_shift).astype(
        jnp.bfloat16
    )


def bias_tile_kernel(pair_ref, gain_ref, shift_ref, weight_ref, mask_ref, tile_ref, total):
    step = pl.program_id(0)
    rows, slots = pair_ref.shape[0], 32
    lane = lax.broadcasted_iota(jnp.int32, (LANES, LANES), 1)
    slot = lax.rem(lane, slots)
    weight = weight_ref[...]
    left, right = [], []
    for row in range(rows):
        left.append(layer_norm(pair_ref[row], gain_ref[...], shift_ref[...]))
        right.append(jnp.where(slot == step * rows + row, weight, 0.0).astype(jnp.bfloat16))
    part = dot(jnp.concatenate(left, 1), jnp.concatenate(right, 0))

    @pl.when(step == 0)
    def _():
        total[...] = part

    @pl.when(step > 0)
    def _():
        total[...] += part

    @pl.when(step == pl.num_programs(0) - 1)
    def _():
        lanes = lax.broadcasted_iota(jnp.int32, total.shape, 1)
        is_mask = lanes == rows * pl.num_programs(0)
        tile_ref[...] = jnp.where(is_mask, mask_ref[...], total[...]).astype(jnp.bfloat16)


def bias_tile(pair, gain, shift, bias_weight, mask, block):
    rows, cols, channels = pair.shape
    spread = jnp.repeat(bias_weight, 32, axis=1).astype(jnp.float32)
    whole = lambda a: pl.BlockSpec(a.shape, lambda i: (0,) * a.ndim)
    mask = mask.astype(jnp.float32).reshape(cols, 1)
    return pl.pallas_call(
        bias_tile_kernel,
        grid=(rows // block,),
        in_specs=[pl.BlockSpec((block, cols, channels), lambda i: (i, 0, 0))]
        + [whole(a) for a in (gain, shift, spread, mask)],
        out_specs=pl.BlockSpec((cols, LANES), lambda i: (0, 0)),
        out_shape=jax.ShapeDtypeStruct((cols, LANES), jnp.bfloat16),
        scratch_shapes=[pltpu.VMEM((cols, LANES), jnp.float32)],
        name="bias_tile",
    )(pair, gain, shift, spread, mask)


def assemble_kernel(index_ref, near_ref, far_ref, order_ref, bias_ref, present_ref, tiles, marks):
    count, cols, _ = near_ref.shape
    tiles[:count] = near_ref[...]
    tiles[count:] = far_ref[...]
    for half in range(2):
        taken = [tiles[index_ref[half * count + place]] for place in range(count)]
        marks[half * cols : (half + 1) * cols] = taken[0].astype(jnp.float32)[:, 24:25]
        bias_ref[half * cols : (half + 1) * cols] = dot(
            jnp.concatenate(taken, 1), order_ref[...]
        )
    present = jnp.max(marks[...])
    present_ref[0, 0] = (present > 0.5).astype(jnp.int32)
    hidden = jnp.logical_and(marks[...] < 0.5, present > 0.5)
    bias_ref[...] = jnp.where(hidden, MISSING, bias_ref[...])


def lane_order(cols, rows, places):
    order = np.zeros((places * LANES, 4 * cols), np.float32)
    for place in range(places):
        for head in range(4):
            for row in range(rows):
                query = place * rows + row
                base = (head // 2) * 2 * cols
                if query < LANES:
                    lane = base + (head % 2) * LANES + query
                else:
                    lane = base + 2 * LANES + (head % 2) * (cols - LANES) + query - LANES
                order[place * LANES + head * 32 + row, lane] = 1
    return jnp.asarray(order, jnp.bfloat16)


def assemble(index, near, far, order):
    count, cols, _ = near.shape
    vmem = pl.BlockSpec(memory_space=pltpu.VMEM)
    smem = pl.BlockSpec(memory_space=pltpu.SMEM)
    return pl.pallas_call(
        assemble_kernel,
        in_specs=[smem, vmem, vmem, vmem],
        out_specs=[vmem, smem],
        out_shape=[
            jax.ShapeDtypeStruct((2 * cols, order.shape[1]), jnp.float32),
            jax.ShapeDtypeStruct((1, 1), jnp.int32),
        ],
        scratch_shapes=[
            pltpu.VMEM((2 * count, cols, LANES), jnp.bfloat16),
            pltpu.VMEM((2 * cols, 1), jnp.float32),
        ],
        compiler_params=pltpu.CompilerParams(vmem_limit_bytes=32 << 20),
        name="assemble_bias",
    )(index, near, far, order)


def project_kernel(own_ref, other_ref, gain_ref, shift_ref, wk_ref, wv_ref, wqg_ref, gb_ref, k_ref, v_ref, q_ref, g_ref):
    for row in range(own_ref.shape[0]):
        own = layer_norm(own_ref[row], gain_ref[...], shift_ref[...])
        other = layer_norm(other_ref[row], gain_ref[...], shift_ref[...])
        both = jnp.concatenate((own, other), 0)
        twice = jnp.concatenate((own, own[LANES:]), 0)
        k_ref[row] = dot(both, wk_ref[...]).astype(jnp.bfloat16)
        v_ref[row] = dot(wv_ref[...], both, NT).astype(jnp.bfloat16)
        mixed = dot(wqg_ref[...], twice, NT)
        q_ref[row] = (mixed[:LANES] * 32 ** (-0.5)).astype(jnp.bfloat16)
        g_ref[row] = 0.5 * jnp.tanh(0.5 * (mixed[LANES:] + gb_ref[...])) + 0.5


def project(own, other, weights, block):
    rows, cols, channels = own.shape
    tile = lambda *shape: pl.BlockSpec((block,) + shape, lambda i: (i, 0, 0))
    whole = lambda a: pl.BlockSpec(a.shape, lambda i: (0,) * a.ndim)
    shape = lambda *s, dtype=jnp.bfloat16: jax.ShapeDtypeStruct((rows,) + s, dtype)
    return pl.pallas_call(
        project_kernel,
        grid=(rows // block,),
        in_specs=[tile(cols, channels)] * 2 + [whole(a) for a in weights],
        out_specs=[
            tile(2 * cols, LANES),
            tile(LANES, 2 * cols),
            tile(LANES, 2 * LANES),
            tile(LANES, 2 * LANES),
        ],
        out_shape=[
            shape(2 * cols, LANES),
            shape(LANES, 2 * cols),
            shape(LANES, 2 * LANES),
            shape(LANES, 2 * LANES, dtype=jnp.float32),
        ],
        compiler_params=pltpu.CompilerParams(vmem_limit_bytes=48 << 20),
        name="project_rows",
    )(own, other, *weights)


TILE_ROWS = ((0, 32), (32, 64), (0, 64), (64, 96), (96, 128), (64, 128))


def attend_kernel(present_ref, k_ref, v_ref, q_ref, g_ref, bias_ref, wo_ref, ob_ref, out_ref, *scratch):
    rows = k_ref.shape[0]
    cols = out_ref.shape[1]
    low = lax.broadcasted_iota(jnp.int32, (32, LANES), 1) < 64
    scores, weights = scratch[0:2], scratch[2:4]
    tops, shares = scratch[4:6], scratch[6:8]
    lanes = [slice(tile * LANES, (tile + 1) * LANES) for tile in range(6)]

    def blank(count):
        return jnp.zeros((count, LANES), jnp.bfloat16)

    def query_tile(row, tile):
        begin, end = TILE_ROWS[tile]
        if tile % 3 < 2:
            part = q_ref[row, begin:end, :LANES]
        else:
            first = q_ref[row, begin : begin + 32, LANES:]
            second = q_ref[row, begin + 32 : end, LANES:]
            part = jnp.concatenate(
                (jnp.where(low, first, 0), jnp.where(low, 0, second)), 0
            ).astype(jnp.bfloat16)
        pieces = [part]
        if begin:
            pieces.insert(0, blank(begin))
        if end < LANES:
            pieces.append(blank(LANES - end))
        return jnp.concatenate(pieces, 0)

    def score(row, slot, shift):
        for tile in range(6):
            part = dot(k_ref[row], query_tile(row, tile)) + bias_ref[:, lanes[tile]]
            if shift:
                part = part + MISSING
            scores[slot][:, lanes[tile]] = part
            tops[slot][0:1, lanes[tile]] = jnp.max(part, axis=0, keepdims=True)
            yield

    def soften(slot):
        for tile in range(6):
            part = jnp.exp(scores[slot][:, lanes[tile]] - tops[slot][0:1, lanes[tile]])
            shares[slot][0:1, lanes[tile]] = 1.0 / jnp.sum(part, axis=0, keepdims=True)
            weights[slot][:, lanes[tile]] = part.astype(jnp.bfloat16)
            yield

    def mix(row, slot):
        mixed = []
        for tile in range(6):
            begin, end = TILE_ROWS[tile]
            part = dot(v_ref[row, begin:end], weights[slot][:, lanes[tile]])
            mixed.append(part * shares[slot][0:1, lanes[tile]])
            yield
        gated = []
        for pair in range(2):
            first, second, third = mixed[3 * pair : 3 * pair + 3]
            gate = g_ref[row, 64 * pair : 64 * pair + 32]
            gated.append(
                jnp.concatenate(
                    (first * gate[:, :LANES], jnp.where(low, third[:32] * gate[:, LANES:], 0.0)), 1
                )
            )
            gate = g_ref[row, 64 * pair + 32 : 64 * pair + 64]
            gated.append(
                jnp.concatenate(
                    (second * gate[:, :LANES], jnp.where(low, 0.0, third[32:] * gate[:, LANES:])), 1
                )
            )
        gated = jnp.concatenate(gated, 0).astype(jnp.bfloat16)
        update = dot(gated, wo_ref[...], TN)
        rest = cols - LANES
        update = jnp.concatenate(
            (update[:LANES], update[LANES : LANES + rest] + update[LANES + rest :]), 0
        )
        out_ref[row] = (update + ob_ref[...]).astype(jnp.bfloat16)
        yield

    def run(*stages):
        stages = list(stages)
        while stages:
            stages = [stage for stage in stages if next(stage, True) is None]

    @pl.when(present_ref[0, 0] > 0)
    def _():
        for step in range(rows + 2):
            stages = []
            if step >= 2:
                stages.append(mix(step - 2, step % 2))
            if 1 <= step <= rows:
                stages.append(soften((step - 1) % 2))
            if step < rows:
                stages.append(score(step, step % 2, False))
            run(*stages)

    @pl.when(present_ref[0, 0] == 0)
    def _():
        def one(row, carry):
            run(score(row, 0, True))
            run(soften(0))
            run(mix(row, 0))
            return carry

        lax.fori_loop(0, rows, one, 0)


def attend(present, k, v, q, g, bias, wo, ob, block):
    rows, keys, _ = k.shape
    cols = keys // 2
    tile = lambda a: pl.BlockSpec((block,) + a.shape[1:], lambda i: (i, 0, 0))
    whole = lambda a: pl.BlockSpec(a.shape, lambda i: (0,) * a.ndim)
    lanes = bias.shape[1]
    return pl.pallas_call(
        attend_kernel,
        grid=(rows // block,),
        in_specs=[pl.BlockSpec(memory_space=pltpu.SMEM)]
        + [tile(a) for a in (k, v, q, g)]
        + [whole(a) for a in (bias, wo, ob)],
        out_specs=pl.BlockSpec((block, cols, LANES), lambda i: (i, 0, 0)),
        out_shape=jax.ShapeDtypeStruct((rows, cols, LANES), jnp.bfloat16),
        scratch_shapes=[pltpu.VMEM((keys, lanes), jnp.float32)] * 2
        + [pltpu.VMEM((keys, lanes), jnp.bfloat16)] * 2
        + [pltpu.VMEM((8, lanes), jnp.float32)] * 4,
        compiler_params=pltpu.CompilerParams(vmem_limit_bytes=56 << 20),
        name="attend_rows",
    )(present, k, v, q, g, bias, wo, ob)


def device(z_hi, z_lo, y, core, x):
    return (((z_hi * 2 + z_lo) * 2 + y) * 2 + core) * 2 + x


def spread_tiles(tile):
    arrived = []
    for t in range(8):
        t0, t1, t2 = t >> 2, (t >> 1) & 1, t & 1
        moves = [
            (device(a, b, y, c, x), device(x ^ t2, b ^ t0, y ^ t1, c, a))
            for a in range(2)
            for b in range(2)
            for y in range(2)
            for c in range(2)
            for x in range(2)
        ]
        arrived.append(lax.ppermute(tile, ("rows", "cols"), moves))
    return jnp.stack(arrived)


def shards_general(
    pair, token_mask, norm_gain, norm_shift, in_weight, gate_bias, bias_weight, out_weight, out_bias
):
    row_count, col_count, channels = pair.shape
    head_count = bias_weight.shape[1]
    inner_width = out_weight.shape[0]
    head_size = inner_width // head_count
    normed = layer_norm(pair, norm_gain, norm_shift)
    flat_normed = normed.reshape(row_count * col_count, channels)
    bias_tile = jnp.einsum(
        "jkc,ch->jhk", normed, bias_weight, preferred_element_type=jnp.float32
    ).astype(jnp.bfloat16)
    bias_columns = lax.all_gather(bias_tile, "rows", axis=0, tiled=True)
    own_bias = lax.all_to_all(bias_columns, "cols", split_axis=0, concat_axis=2, tiled=True)
    query_gate = jnp.concatenate(
        (in_weight[:, :inner_width], in_weight[:, 3 * inner_width :]), axis=1
    )
    projected = jnp.dot(flat_normed, query_gate, preferred_element_type=jnp.float32)
    queries = (projected[:, :inner_width] * head_size ** (-0.5)).astype(jnp.bfloat16)
    queries = queries.reshape(row_count, col_count, head_count, head_size)
    gates = jax.nn.sigmoid(projected[:, inner_width:] + gate_bias)
    key_value_weight = in_weight[:, inner_width : 3 * inner_width]
    mask_row = token_mask.reshape(1, col_count)
    start_state = (
        jnp.full((row_count, col_count, head_count), -jnp.inf, jnp.float32),
        jnp.zeros((row_count, col_count, head_count), jnp.float32),
        jnp.zeros((row_count, col_count, inner_width), jnp.float32),
    )
    key_values = jnp.dot(flat_normed, key_value_weight, preferred_element_type=jnp.float32).astype(
        jnp.bfloat16
    )
    key_values = key_values.reshape(row_count, col_count, 2 * inner_width)
    pair_keys = lax.all_gather(key_values, "cols", axis=1, tiled=True)
    mask_in = lax.all_gather(mask_row, "cols", axis=1, tiled=True)
    state_now = start_state
    begin_at = jnp.int32(0)
    span_len = pair_keys.shape[1]
    for low_edge in range(0, span_len, col_count):
        high_edge = min(low_edge + col_count, span_len)
        attend_pair_keys = pair_keys[:, low_edge:high_edge]
        attend_begin_at = begin_at + low_edge
        attend_running_max, attend_totals, attend_summed = state_now
        attend_span_len = attend_pair_keys.shape[1]
        key_part = attend_pair_keys[..., :inner_width].reshape(
            row_count, attend_span_len, head_count, head_size
        )
        value_part = attend_pair_keys[..., inner_width:].reshape(
            row_count, attend_span_len, head_count, head_size
        )
        scores = jnp.einsum(
            "rjhd,rkhd->rjhk", queries, key_part, preferred_element_type=jnp.float32
        )
        bias_part = lax.dynamic_slice_in_dim(own_bias, attend_begin_at, attend_span_len, 2).astype(
            jnp.float32
        )
        masking = 1000000000.0 * (mask_in[:, low_edge:high_edge][0].astype(jnp.float32) - 1.0)
        scores = scores + bias_part + masking
        new_max = jnp.maximum(attend_running_max, jnp.max(scores, axis=-1))
        shrink = jnp.exp(attend_running_max - new_max)
        weights = jnp.exp(scores - new_max[..., None])
        attend_totals = attend_totals * shrink + jnp.sum(weights, axis=-1)
        mixed_part = jnp.einsum(
            "rjhk,rkhd->rjhd",
            weights.astype(jnp.bfloat16),
            value_part,
            preferred_element_type=jnp.float32,
        )
        attend_summed = (
            attend_summed.reshape(row_count, col_count, head_count, head_size) * shrink[..., None]
            + mixed_part
        )
        state_now = (
            new_max,
            attend_totals,
            attend_summed.reshape(row_count, col_count, inner_width),
        )
    running_max, totals, summed = state_now
    attended = summed.reshape(row_count, col_count, head_count, head_size) / totals[..., None]
    gated = gates.reshape(row_count, col_count, head_count, head_size) * attended
    gated = gated.astype(jnp.bfloat16).reshape(row_count * col_count, inner_width)
    updated = jnp.dot(gated, out_weight, preferred_element_type=jnp.float32) + out_bias
    return updated.astype(jnp.bfloat16).reshape(row_count, col_count, channels)


def fits(mesh, pair_shape, heads, inner):
    rows, cols, channels = pair_shape
    return (
        (mesh.shape["rows"], mesh.shape["cols"]) == (16, 2)
        and (rows, cols, channels) == (24, 192, LANES)
        and (heads, inner) == (4, LANES)
    )


def shards(
    pair, token_mask, norm_gain, norm_shift, in_weight, gate_bias, bias_weight, out_weight, out_bias
):
    rows, cols, channels = pair.shape
    inner = out_weight.shape[0]
    gain, shift = norm_gain.reshape(1, channels), norm_shift.reshape(1, channels)
    step = rows // CHUNKS
    swap = [(0, 1), (1, 0)]
    parts = [pair[i * step : (i + 1) * step] for i in range(CHUNKS)]
    others = [lax.ppermute(part, "cols", swap) for part in parts]
    tile = bias_tile(pair, gain, shift, bias_weight, token_mask, step)
    near = spread_tiles(tile)
    far = lax.ppermute(near, "rows", [(i, i ^ 1) for i in range(16)])
    row = lax.axis_index("rows")
    x = lax.axis_index("cols")
    z_hi, z_lo, y, core = row >> 3, (row >> 2) & 1, (row >> 1) & 1, row & 1
    place = jnp.arange(16, dtype=jnp.int32)
    half, a, b, c = place >> 3, (place >> 2) & 1, (place >> 1) & 1, place & 1
    index = (c ^ core) * 8 + (a ^ z_lo) * 4 + (b ^ y) * 2 + (half ^ z_hi ^ x)
    bias, present = assemble(index, near, far, lane_order(cols, rows, 8))
    weights = (
        gain,
        shift,
        in_weight[:, inner : 2 * inner],
        in_weight[:, 2 * inner : 3 * inner].T,
        jnp.concatenate((in_weight[:, :inner].T, in_weight[:, 3 * inner :].T), 0),
        gate_bias.reshape(inner, 1),
    )
    outs = []
    for part, other in zip(parts, others):
        k, v, q, g = project(part, other, weights, step // 2)
        outs.append(attend(present, k, v, q, g, bias, out_weight, out_bias.reshape(1, channels), step))
    return jnp.concatenate(outs, 0)


def solution(mesh):
    placed = (P("rows", "cols", None), P("cols"), P(), P(), P(), P(), P(), P(), P())

    def run(pair, *rest):
        tall, wide, channels = pair.shape
        block = (tall // mesh.shape["rows"], wide // mesh.shape["cols"], channels)
        bias_weight, out_weight = rest[5], rest[6]
        special = fits(mesh, block, bias_weight.shape[1], out_weight.shape[0])
        return jax.shard_map(
            shards if special else shards_general,
            mesh=mesh,
            in_specs=placed,
            out_specs=P("rows", "cols", None),
            check_vma=False,
        )(pair, *rest)

    return run
```

```python
import functools

import jax
import jax.numpy as jnp
import numpy as np
from jax import lax
from jax.experimental import pallas as pl
from jax.experimental.pallas import tpu as pltpu
from jax.sharding import PartitionSpec as P

LANES = 128
MISSING = -1e9
NN = (((1,), (0,)), ((), ()))
NT = (((1,), (1,)), ((), ()))
TN = (((0,), (0,)), ((), ()))
CHUNKS = ((0, 8), (8, 8), (16, 8))
VMEM = 14 << 20
ALL_VMEM = 60 << 20


def dot(left, right, dims=NN):
    return lax.dot_general(left, right, dims, preferred_element_type=jnp.float32)


def layer_norm(pair_block, norm_gain, norm_shift):
    as_float = pair_block.astype(jnp.float32)
    center = jnp.mean(as_float, axis=-1, keepdims=True)
    spread = jnp.mean(jnp.square(as_float - center), axis=-1, keepdims=True)
    return ((as_float - center) * lax.rsqrt(spread + 1e-05) * norm_gain + norm_shift).astype(
        jnp.bfloat16
    )


def normed_rows(block, mean_weight, gain, shift):
    center = block.astype(jnp.float32) - dot(block, mean_weight)
    spread = jnp.mean(center * center, axis=-1, keepdims=True)
    return (center * lax.rsqrt(spread + 1e-05) * gain + shift).astype(jnp.bfloat16)


def norm_kernel(pair_ref, gain_ref, shift_ref, weight_ref, mask_ref, normed_ref, tile_ref, total, wide):
    step = pl.program_id(0)
    rows, slots = pair_ref.shape[0], 32
    lane = lax.broadcasted_iota(jnp.int32, (LANES, LANES), 1)

    @pl.when(step == 0)
    def _():
        heads = weight_ref.shape[0]
        head = lax.broadcasted_iota(jnp.int32, (heads, LANES), 0)
        place = lax.broadcasted_iota(jnp.int32, (heads, LANES), 1)
        begin = head * slots
        expand = jnp.logical_and(place >= begin, place < begin + slots)
        wide[...] = dot(weight_ref[...], expand.astype(jnp.bfloat16), TN)
        spot = lax.broadcasted_iota(jnp.int32, (1, LANES), 1) == rows * pl.num_programs(0)
        total[...] = dot(mask_ref[...].astype(jnp.bfloat16), spot.astype(jnp.bfloat16), TN)

    slot = lax.rem(lane, slots)
    mean_weight = jnp.full((LANES, LANES), 1 / LANES, jnp.bfloat16)
    left, right = [], []
    for row in range(rows):
        normed = normed_rows(pair_ref[row], mean_weight, gain_ref[...], shift_ref[...])
        normed_ref[row] = normed
        left.append(normed)
        right.append(jnp.where(slot == step * rows + row, wide[...], 0.0).astype(jnp.bfloat16))
    total[...] += dot(jnp.concatenate(left, 1), jnp.concatenate(right, 0))

    @pl.when(step == pl.num_programs(0) - 1)
    def _():
        tile_ref[...] = total[...].astype(jnp.bfloat16)


def norm_and_tile(pair, gain, shift, bias_weight, mask, block):
    rows, cols, channels = pair.shape
    whole = lambda a: pl.BlockSpec(a.shape, lambda i: (0,) * a.ndim)
    small = (gain, shift, bias_weight.T, mask.reshape(1, cols))
    rows_spec = pl.BlockSpec((block, cols, channels), lambda i: (i, 0, 0))
    return pl.pallas_call(
        norm_kernel,
        grid=(rows // block,),
        in_specs=[rows_spec] + [whole(a) for a in small],
        out_specs=[rows_spec, pl.BlockSpec((cols, LANES), lambda i: (0, 0))],
        out_shape=[
            jax.ShapeDtypeStruct(pair.shape, jnp.bfloat16),
            jax.ShapeDtypeStruct((cols, LANES), jnp.bfloat16),
        ],
        scratch_shapes=[
            pltpu.VMEM((cols, LANES), jnp.float32),
            pltpu.VMEM((channels, LANES), jnp.float32),
        ],
        compiler_params=pltpu.CompilerParams(vmem_limit_bytes=ALL_VMEM),
        cost_estimate=pl.CostEstimate(flops=10**9, bytes_accessed=10**7, transcendentals=0),
        name="norm_and_tile",
    )(pair, *small)


def assemble_kernel(index_ref, near_ref, far_ref, order_ref, bias_ref, tiles, marks):
    count, cols, _ = near_ref.shape
    tiles[:count] = near_ref[...]
    tiles[count:] = far_ref[...]
    for half in range(2):
        taken = [tiles[index_ref[half * count + place]] for place in range(count)]
        marks[half * cols : (half + 1) * cols] = taken[0].astype(jnp.float32)[:, 24:25]
        bias_ref[half * cols : (half + 1) * cols] = dot(
            jnp.concatenate(taken, 1), order_ref[...]
        )
    present = jnp.max(marks[...], axis=0, keepdims=True)
    hidden = jnp.logical_and(marks[...] < 0.5, present > 0.5)
    bias_ref[: 2 * cols] = jnp.where(hidden, MISSING, bias_ref[: 2 * cols])
    bias_ref[2 * cols :] = jnp.broadcast_to(present, (8, bias_ref.shape[1]))


def lane_order(cols, rows, places):
    order = np.zeros((places * LANES, 4 * cols), np.float32)
    for place in range(places):
        for head in range(4):
            for row in range(rows):
                query = place * rows + row
                base = (head // 2) * 2 * cols
                if query < LANES:
                    lane = base + (head % 2) * LANES + query
                else:
                    lane = base + 2 * LANES + (head % 2) * (cols - LANES) + query - LANES
                order[place * LANES + head * 32 + row, lane] = 1
    return jnp.asarray(order, jnp.bfloat16)


def assemble(index, near, far, order):
    count, cols, _ = near.shape
    vmem = pl.BlockSpec(memory_space=pltpu.VMEM)
    smem = pl.BlockSpec(memory_space=pltpu.SMEM)
    return pl.pallas_call(
        assemble_kernel,
        in_specs=[smem, vmem, vmem, vmem],
        out_specs=vmem,
        out_shape=jax.ShapeDtypeStruct((2 * cols + 8, order.shape[1]), jnp.float32),
        scratch_shapes=[
            pltpu.VMEM((2 * count, cols, LANES), jnp.bfloat16),
            pltpu.VMEM((2 * cols, 1), jnp.float32),
        ],
        compiler_params=pltpu.CompilerParams(vmem_limit_bytes=VMEM),
        cost_estimate=pl.CostEstimate(flops=10**9, bytes_accessed=4 * 10**6, transcendentals=0),
        name="assemble_bias",
    )(index, near, far, order)


def project_kernel(own_ref, wk_ref, wv_ref, wqg_ref, gb_ref, k_ref, v_ref, q_ref, g_ref):
    rows, cols, channels = own_ref.shape
    keys = dot(own_ref[...].reshape(rows * cols, channels), wk_ref[...])
    k_ref[...] = keys.astype(jnp.bfloat16).reshape(k_ref.shape)
    for row in range(rows):
        own = own_ref[row]
        v_ref[row] = dot(wv_ref[...], own, NT).astype(jnp.bfloat16)
        mixed = dot(wqg_ref[...], jnp.concatenate((own, own[LANES:]), 0), NT)
        q_ref[row] = (mixed[:LANES] * 32 ** (-0.5)).astype(jnp.bfloat16)
        g_ref[row] = 0.5 * jnp.tanh(0.5 * (mixed[LANES:] + gb_ref[...])) + 0.5


def project(normed, weights, block):
    rows, cols, channels = normed.shape
    tile = lambda *shape: pl.BlockSpec((block,) + shape, lambda i: (i, 0, 0))
    whole = lambda a: pl.BlockSpec(a.shape, lambda i: (0,) * a.ndim)
    sizes = ((cols, LANES), (LANES, cols), (LANES, 2 * LANES), (LANES, 2 * LANES))
    kinds = (jnp.bfloat16,) * 3 + (jnp.float32,)
    return pl.pallas_call(
        project_kernel,
        grid=(rows // block,),
        in_specs=[tile(cols, channels)] + [whole(a) for a in weights],
        out_specs=[tile(*size) for size in sizes],
        out_shape=[jax.ShapeDtypeStruct((rows,) + size, kind) for size, kind in zip(sizes, kinds)],
        compiler_params=pltpu.CompilerParams(vmem_limit_bytes=VMEM),
        cost_estimate=pl.CostEstimate(flops=10**9, bytes_accessed=10**7, transcendentals=0),
        name="project_own",
    )(normed, *weights)


TILE_ROWS = ((0, 32), (32, 64), (0, 64), (64, 96), (96, 128), (64, 128))


def attend_kernel(begin, first, *refs):
    if not first:
        refs = refs[1:]
    other_ref, k_ref, v_ref, q_ref, g_ref, bias_ref, wk_ref, wv_ref, wo_ref, ob_ref, out_ref = refs[:11]
    k_other, v_both, *scratch = refs[11:]
    scores, weights, tops, shares = (scratch[2 * n : 2 * n + 2] for n in range(4))
    rows, cols, _ = other_ref.shape
    keys = 2 * cols
    low = lax.broadcasted_iota(jnp.int32, (32, LANES), 1) < 64
    lanes = [slice(tile * LANES, (tile + 1) * LANES) for tile in range(6)]

    def blank(count):
        return jnp.zeros((count, LANES), jnp.bfloat16)

    def query_tile(row, tile):
        head, tail = TILE_ROWS[tile]
        if tile % 3 < 2:
            part = q_ref[begin + row, head:tail, :LANES]
        else:
            one = q_ref[begin + row, head : head + 32, LANES:]
            two = q_ref[begin + row, head + 32 : tail, LANES:]
            part = jnp.concatenate(
                (jnp.where(low, one, 0), jnp.where(low, 0, two)), 0
            ).astype(jnp.bfloat16)
        pieces = [part]
        if head:
            pieces.insert(0, blank(head))
        if tail < LANES:
            pieces.append(blank(LANES - tail))
        return jnp.concatenate(pieces, 0)

    def widen(row):
        other = other_ref[row]
        k_other[row] = dot(other, wk_ref[...]).astype(jnp.bfloat16)
        yield
        values = dot(wv_ref[...], other, NT).astype(jnp.bfloat16)
        v_both[row] = jnp.concatenate((v_ref[begin + row], values), 1)
        yield

    def score(row, slot, shift):
        for tile in range(6):
            query = query_tile(row, tile)
            both = jnp.concatenate((k_ref[begin + row], k_other[row]), 0)
            part = dot(both, query) + bias_ref[:keys, lanes[tile]]
            if shift:
                part = part + MISSING
            scores[slot][:, lanes[tile]] = part
            tops[slot][0:1, lanes[tile]] = jnp.max(part, axis=0, keepdims=True)
            yield

    def soften(slot):
        for tile in range(6):
            part = jnp.exp(scores[slot][:, lanes[tile]] - tops[slot][0:1, lanes[tile]])
            shares[slot][0:1, lanes[tile]] = 1.0 / jnp.sum(part, axis=0, keepdims=True)
            weights[slot][:, lanes[tile]] = part.astype(jnp.bfloat16)
            yield

    def mix(row, slot):
        mixed = []
        for tile in range(6):
            head, tail = TILE_ROWS[tile]
            part = dot(v_both[row, head:tail], weights[slot][:, lanes[tile]])
            mixed.append(part * shares[slot][0:1, lanes[tile]])
            yield
        gated = []
        for pair in range(2):
            one, two, both = mixed[3 * pair : 3 * pair + 3]
            gate = g_ref[begin + row, 64 * pair : 64 * pair + 32]
            rest = jnp.where(low, both[:32] * gate[:, LANES:], 0.0)
            gated.append(jnp.concatenate((one * gate[:, :LANES], rest), 1))
            gate = g_ref[begin + row, 64 * pair + 32 : 64 * pair + 64]
            rest = jnp.where(low, 0.0, both[32:] * gate[:, LANES:])
            gated.append(jnp.concatenate((two * gate[:, :LANES], rest), 1))
        update = dot(jnp.concatenate(gated, 0).astype(jnp.bfloat16), wo_ref[...], TN)
        rest = cols - LANES
        update = jnp.concatenate(
            (update[:LANES], update[LANES : LANES + rest] + update[LANES + rest :]), 0
        )
        out_ref[row] = (update + ob_ref[...]).astype(jnp.bfloat16)
        yield

    def run(*stages):
        stages = list(stages)
        while stages:
            stages = [stage for stage in stages if next(stage, True) is None]

    present = bias_ref[keys, 0]

    @pl.when(present > 0.5)
    def _():
        run(widen(0))
        for step in range(rows + 2):
            stages = []
            if step >= 2:
                stages.append(mix(step - 2, step % 2))
            if 1 <= step <= rows:
                stages.append(soften((step - 1) % 2))
            if step < rows:
                stages.append(score(step, step % 2, False))
            if step + 1 < rows:
                stages.append(widen(step + 1))
            run(*stages)

    @pl.when(present <= 0.5)
    def _():
        for row in range(rows):
            run(widen(row))
            run(score(row, 0, True))
            run(soften(0))
            run(mix(row, 0))


def attend(other, k, v, q, g, bias, wk, wv, wo, ob, out, begin):
    rows, cols, channels = other.shape
    total, keys = k.shape[0], 2 * cols
    lanes = bias.shape[1]
    extra = [] if out is None else [out]
    vmem = pl.BlockSpec(memory_space=pltpu.VMEM)
    return pl.pallas_call(
        functools.partial(attend_kernel, begin, out is None),
        grid=(1,),
        in_specs=[pl.BlockSpec(memory_space=pl.ANY)] * len(extra) + [vmem] * 10,
        out_specs=pl.BlockSpec((rows, cols, LANES), lambda i: (begin // rows, 0, 0)),
        out_shape=jax.ShapeDtypeStruct((total, cols, LANES), jnp.bfloat16),
        scratch_shapes=[
            pltpu.VMEM((rows, cols, LANES), jnp.bfloat16),
            pltpu.VMEM((rows, LANES, keys), jnp.bfloat16),
        ]
        + [pltpu.VMEM((keys, lanes), jnp.float32)] * 2
        + [pltpu.VMEM((keys, lanes), jnp.bfloat16)] * 2
        + [pltpu.VMEM((8, lanes), jnp.float32)] * 4,
        input_output_aliases={0: 0} if extra else {},
        compiler_params=pltpu.CompilerParams(vmem_limit_bytes=24 << 20),
        cost_estimate=pl.CostEstimate(
            flops=10**10, bytes_accessed=10**7, transcendentals=rows * keys * lanes
        ),
        name="attend_rows",
    )(*extra, other, k, v, q, g, bias, wk, wv, wo, ob)


def device(z_hi, z_lo, y, core, x):
    return (((z_hi * 2 + z_lo) * 2 + y) * 2 + core) * 2 + x


def moved(array, move):
    pairs = []
    for number in range(32):
        a, b, y, c, x = ((number >> bit) & 1 for bit in (4, 3, 2, 1, 0))
        target = move(a, b, y, c, x)
        if target is not None:
            pairs.append((number, device(*target)))
    return lax.ppermute(array, ("rows", "cols"), pairs)


def spread_tiles(tile, z_hi, x):
    straight = moved(tile, lambda a, b, y, c, x: (1 - a, b, y, c, x) if a == x else (a, b, y, c, 1 - x))
    across = moved(tile, lambda a, b, y, c, x: None if a == x else (1 - a, b, y, c, 1 - x))
    home = z_hi == x
    pair = jnp.stack((jnp.where(home, tile, straight), jnp.where(home, straight, across)))
    near = [pair]
    for move in (
        lambda a, b, y, c, x: (a, b, 1 - y, c, x),
        lambda a, b, y, c, x: (a, 1 - b, y, c, x),
        lambda a, b, y, c, x: (a, 1 - b, 1 - y, c, x),
    ):
        near.append(moved(pair, move))
    near = jnp.concatenate(near, 0)
    return near, moved(near, lambda a, b, y, c, x: (a, b, y, 1 - c, x))


def shards_general(
    pair, token_mask, norm_gain, norm_shift, in_weight, gate_bias, bias_weight, out_weight, out_bias
):
    row_count, col_count, channels = pair.shape
    head_count = bias_weight.shape[1]
    inner_width = out_weight.shape[0]
    head_size = inner_width // head_count
    normed = layer_norm(pair, norm_gain, norm_shift)
    flat_normed = normed.reshape(row_count * col_count, channels)
    bias_tile = jnp.einsum(
        "jkc,ch->jhk", normed, bias_weight, preferred_element_type=jnp.float32
    ).astype(jnp.bfloat16)
    bias_columns = lax.all_gather(bias_tile, "rows", axis=0, tiled=True)
    own_bias = lax.all_to_all(bias_columns, "cols", split_axis=0, concat_axis=2, tiled=True)
    query_gate = jnp.concatenate(
        (in_weight[:, :inner_width], in_weight[:, 3 * inner_width :]), axis=1
    )
    projected = jnp.dot(flat_normed, query_gate, preferred_element_type=jnp.float32)
    queries = (projected[:, :inner_width] * head_size ** (-0.5)).astype(jnp.bfloat16)
    queries = queries.reshape(row_count, col_count, head_count, head_size)
    gates = jax.nn.sigmoid(projected[:, inner_width:] + gate_bias)
    key_value_weight = in_weight[:, inner_width : 3 * inner_width]
    mask_row = token_mask.reshape(1, col_count)
    start_state = (
        jnp.full((row_count, col_count, head_count), -jnp.inf, jnp.float32),
        jnp.zeros((row_count, col_count, head_count), jnp.float32),
        jnp.zeros((row_count, col_count, inner_width), jnp.float32),
    )
    key_values = jnp.dot(flat_normed, key_value_weight, preferred_element_type=jnp.float32).astype(
        jnp.bfloat16
    )
    key_values = key_values.reshape(row_count, col_count, 2 * inner_width)
    pair_keys = lax.all_gather(key_values, "cols", axis=1, tiled=True)
    mask_in = lax.all_gather(mask_row, "cols", axis=1, tiled=True)
    state_now = start_state
    begin_at = jnp.int32(0)
    span_len = pair_keys.shape[1]
    for low_edge in range(0, span_len, col_count):
        high_edge = min(low_edge + col_count, span_len)
        attend_pair_keys = pair_keys[:, low_edge:high_edge]
        attend_begin_at = begin_at + low_edge
        attend_running_max, attend_totals, attend_summed = state_now
        attend_span_len = attend_pair_keys.shape[1]
        key_part = attend_pair_keys[..., :inner_width].reshape(
            row_count, attend_span_len, head_count, head_size
        )
        value_part = attend_pair_keys[..., inner_width:].reshape(
            row_count, attend_span_len, head_count, head_size
        )
        scores = jnp.einsum(
            "rjhd,rkhd->rjhk", queries, key_part, preferred_element_type=jnp.float32
        )
        bias_part = lax.dynamic_slice_in_dim(own_bias, attend_begin_at, attend_span_len, 2).astype(
            jnp.float32
        )
        masking = 1000000000.0 * (mask_in[:, low_edge:high_edge][0].astype(jnp.float32) - 1.0)
        scores = scores + bias_part + masking
        new_max = jnp.maximum(attend_running_max, jnp.max(scores, axis=-1))
        shrink = jnp.exp(attend_running_max - new_max)
        weights = jnp.exp(scores - new_max[..., None])
        attend_totals = attend_totals * shrink + jnp.sum(weights, axis=-1)
        mixed_part = jnp.einsum(
            "rjhk,rkhd->rjhd",
            weights.astype(jnp.bfloat16),
            value_part,
            preferred_element_type=jnp.float32,
        )
        attend_summed = (
            attend_summed.reshape(row_count, col_count, head_count, head_size) * shrink[..., None]
            + mixed_part
        )
        state_now = (
            new_max,
            attend_totals,
            attend_summed.reshape(row_count, col_count, inner_width),
        )
    running_max, totals, summed = state_now
    attended = summed.reshape(row_count, col_count, head_count, head_size) / totals[..., None]
    gated = gates.reshape(row_count, col_count, head_count, head_size) * attended
    gated = gated.astype(jnp.bfloat16).reshape(row_count * col_count, inner_width)
    updated = jnp.dot(gated, out_weight, preferred_element_type=jnp.float32) + out_bias
    return updated.astype(jnp.bfloat16).reshape(row_count, col_count, channels)


def fits(mesh, pair_shape, heads, inner):
    rows, cols, channels = pair_shape
    return (
        (mesh.shape["rows"], mesh.shape["cols"]) == (16, 2)
        and (rows, cols, channels) == (24, 192, LANES)
        and (heads, inner) == (4, LANES)
    )


def shards(
    pair, token_mask, norm_gain, norm_shift, in_weight, gate_bias, bias_weight, out_weight, out_bias
):
    rows, cols, channels = pair.shape
    inner = out_weight.shape[0]
    gain, shift = norm_gain.reshape(1, channels), norm_shift.reshape(1, channels)
    swap = [(0, 1), (1, 0)]
    normed, tile = norm_and_tile(pair, gain, shift, bias_weight, token_mask, 12)
    row = lax.axis_index("rows")
    x = lax.axis_index("cols")
    z_hi, z_lo, y, core = row >> 3, (row >> 2) & 1, (row >> 1) & 1, row & 1
    near, far = spread_tiles(tile, z_hi, x)
    others = [lax.ppermute(normed[begin : begin + count], "cols", swap) for begin, count in CHUNKS]
    place = jnp.arange(16, dtype=jnp.int32)
    half, a, b, c = place >> 3, (place >> 2) & 1, (place >> 1) & 1, place & 1
    index = (c ^ core) * 8 + (a ^ z_lo) * 4 + (b ^ y) * 2 + half
    bias = assemble(index, near, far, lane_order(cols, rows, 8))
    wk, wv = in_weight[:, inner : 2 * inner], in_weight[:, 2 * inner : 3 * inner].T
    wqg = jnp.concatenate((in_weight[:, :inner].T, in_weight[:, 3 * inner :].T), 0)
    own = project(normed, (wk, wv, wqg, gate_bias.reshape(inner, 1)), 8)
    out = None
    for (begin, count), other in zip(CHUNKS, others):
        if out is not None:
            other, out = lax.optimization_barrier((other, out))
        out = attend(
            other, *own, bias, wk, wv, out_weight, out_bias.reshape(1, channels), out, begin
        )
    return out


def solution(mesh):
    placed = (P("rows", "cols", None), P("cols"), P(), P(), P(), P(), P(), P(), P())

    def run(pair, *rest):
        tall, wide, channels = pair.shape
        block = (tall // mesh.shape["rows"], wide // mesh.shape["cols"], channels)
        bias_weight, out_weight = rest[5], rest[6]
        special = fits(mesh, block, bias_weight.shape[1], out_weight.shape[0])
        return jax.shard_map(
            shards if special else shards_general,
            mesh=mesh,
            in_specs=placed,
            out_specs=P("rows", "cols", None),
            check_vma=False,
        )(pair, *rest)

    return run
```

```python
import functools

import jax
import jax.numpy as jnp
import numpy as np
from jax import lax
from jax.experimental import pallas as pl
from jax.experimental.pallas import tpu as pltpu
from jax.sharding import PartitionSpec as P

LANES = 128
MISSING = -1e9
NN = (((1,), (0,)), ((), ()))
NT = (((1,), (1,)), ((), ()))
TN = (((0,), (0,)), ((), ()))
CHUNKS = ((0, 8), (8, 8), (16, 8))
VMEM = 14 << 20
ALL_VMEM = 60 << 20


def dot(left, right, dims=NN):
    return lax.dot_general(left, right, dims, preferred_element_type=jnp.float32)


def layer_norm(pair_block, norm_gain, norm_shift):
    as_float = pair_block.astype(jnp.float32)
    center = jnp.mean(as_float, axis=-1, keepdims=True)
    spread = jnp.mean(jnp.square(as_float - center), axis=-1, keepdims=True)
    return ((as_float - center) * lax.rsqrt(spread + 1e-05) * norm_gain + norm_shift).astype(
        jnp.bfloat16
    )


def normed_rows(block, mean_weight, gain, shift):
    center = block.astype(jnp.float32) - dot(block, mean_weight)
    spread = jnp.mean(center * center, axis=-1, keepdims=True)
    return (center * lax.rsqrt(spread + 1e-05) * gain + shift).astype(jnp.bfloat16)


def norm_kernel(parts, pair_hbm, *refs):
    small_hbm, refs = refs[:4], refs[4:]
    normed_refs, tile_ref, refs = refs[: len(parts)], refs[len(parts)], refs[len(parts) + 1 :]
    pair_ref, gain_ref, shift_ref, weight_ref, mask_ref, done = refs
    rows, slots = pair_ref.shape[0], 32
    copies = [
        pltpu.make_async_copy(source, target, done.at[place])
        for place, (source, target) in enumerate(
            zip(small_hbm, (gain_ref, shift_ref, weight_ref, mask_ref))
        )
    ]
    for place, (begin, count) in enumerate(parts):
        block = pl.ds(begin, count)
        copies.append(
            pltpu.make_async_copy(pair_hbm.at[block], pair_ref.at[block], done.at[4 + place])
        )
    for copy in copies:
        copy.start()
    for copy in copies[:4]:
        copy.wait()

    heads = weight_ref.shape[0]
    head = lax.broadcasted_iota(jnp.int32, (heads, LANES), 0)
    place = lax.broadcasted_iota(jnp.int32, (heads, LANES), 1)
    expand = jnp.logical_and(place >= head * slots, place < head * slots + slots)
    wide = dot(weight_ref[...], expand.astype(jnp.bfloat16), TN)
    spot = lax.broadcasted_iota(jnp.int32, (1, LANES), 1) == rows
    total = dot(mask_ref[...].astype(jnp.bfloat16), spot.astype(jnp.bfloat16), TN)
    slot = lax.rem(lax.broadcasted_iota(jnp.int32, (LANES, LANES), 1), slots)
    mean_weight = jnp.full((LANES, LANES), 1 / LANES, jnp.bfloat16)
    for (begin, count), copy, normed_ref in zip(parts, copies[4:], normed_refs):
        copy.wait()
        left, right = [], []
        for row in range(begin, begin + count):
            normed = normed_rows(pair_ref[row], mean_weight, gain_ref[...], shift_ref[...])
            normed_ref[row - begin] = normed
            left.append(normed)
            right.append(jnp.where(slot == row, wide, 0.0).astype(jnp.bfloat16))
        total += dot(jnp.concatenate(left, 1), jnp.concatenate(right, 0))
    tile_ref[...] = total.astype(jnp.bfloat16)


def norm_and_tile(pair, gain, shift, bias_weight, mask, parts):
    rows, cols, channels = pair.shape
    small = (gain, shift, bias_weight.T, mask.reshape(1, cols))
    vmem = pl.BlockSpec(memory_space=pltpu.VMEM)
    return pl.pallas_call(
        functools.partial(norm_kernel, parts),
        in_specs=[pl.BlockSpec(memory_space=pltpu.HBM)] * 5,
        out_specs=[vmem] * (len(parts) + 1),
        out_shape=[
            jax.ShapeDtypeStruct((count, cols, channels), jnp.bfloat16) for _, count in parts
        ]
        + [jax.ShapeDtypeStruct((cols, LANES), jnp.bfloat16)],
        scratch_shapes=[pltpu.VMEM(pair.shape, pair.dtype)]
        + [pltpu.VMEM(a.shape, a.dtype) for a in small]
        + [pltpu.SemaphoreType.DMA((4 + len(parts),))],
        compiler_params=pltpu.CompilerParams(vmem_limit_bytes=ALL_VMEM),
        cost_estimate=pl.CostEstimate(flops=10**9, bytes_accessed=10**7, transcendentals=0),
        name="norm_and_tile",
    )(pair, *small)


def assemble_kernel(index_ref, near_ref, far_ref, order_ref, bias_ref, tiles, marks):
    count, cols, _ = near_ref.shape
    tiles[:count] = near_ref[...]
    tiles[count:] = far_ref[...]
    for half in range(2):
        taken = [tiles[index_ref[half * count + place]] for place in range(count)]
        marks[half * cols : (half + 1) * cols] = taken[0].astype(jnp.float32)[:, 24:25]
        bias_ref[half * cols : (half + 1) * cols] = dot(
            jnp.concatenate(taken, 1), order_ref[...]
        )
    present = jnp.max(marks[...], axis=0, keepdims=True)
    hidden = jnp.logical_and(marks[...] < 0.5, present > 0.5)
    bias_ref[: 2 * cols] = jnp.where(hidden, MISSING, bias_ref[: 2 * cols])
    bias_ref[2 * cols :] = jnp.broadcast_to(present, (8, bias_ref.shape[1]))


def lane_order(cols, rows, places):
    order = np.zeros((places * LANES, 4 * cols), np.float32)
    for place in range(places):
        for head in range(4):
            for row in range(rows):
                query = place * rows + row
                base = (head // 2) * 2 * cols
                if query < LANES:
                    lane = base + (head % 2) * LANES + query
                else:
                    lane = base + 2 * LANES + (head % 2) * (cols - LANES) + query - LANES
                order[place * LANES + head * 32 + row, lane] = 1
    return jnp.asarray(order, jnp.bfloat16)


def assemble(index, near, far, order):
    count, cols, _ = near.shape
    vmem = pl.BlockSpec(memory_space=pltpu.VMEM)
    smem = pl.BlockSpec(memory_space=pltpu.SMEM)
    return pl.pallas_call(
        assemble_kernel,
        in_specs=[smem, vmem, vmem, vmem],
        out_specs=vmem,
        out_shape=jax.ShapeDtypeStruct((2 * cols + 8, order.shape[1]), jnp.float32),
        scratch_shapes=[
            pltpu.VMEM((2 * count, cols, LANES), jnp.bfloat16),
            pltpu.VMEM((2 * cols, 1), jnp.float32),
        ],
        compiler_params=pltpu.CompilerParams(vmem_limit_bytes=VMEM),
        cost_estimate=pl.CostEstimate(flops=10**9, bytes_accessed=4 * 10**6, transcendentals=0),
        name="assemble_bias",
    )(index, near, far, order)


def project_kernel(count, *refs):
    own_refs, refs = refs[:count], refs[count:]
    wk_ref, wv_ref, wqg_ref, gb_ref, k_ref, v_ref, q_ref, g_ref = refs
    begin = 0
    for own_ref in own_refs:
        rows, cols, channels = own_ref.shape
        keys = dot(own_ref[...].reshape(rows * cols, channels), wk_ref[...])
        k_ref[begin : begin + rows] = keys.astype(jnp.bfloat16).reshape(rows, cols, LANES)
        for row in range(rows):
            own = own_ref[row]
            v_ref[begin + row] = dot(wv_ref[...], own, NT).astype(jnp.bfloat16)
            mixed = dot(wqg_ref[...], jnp.concatenate((own, own[LANES:]), 0), NT)
            q_ref[begin + row] = (mixed[:LANES] * 32 ** (-0.5)).astype(jnp.bfloat16)
            g_ref[begin + row] = 0.5 * jnp.tanh(0.5 * (mixed[LANES:] + gb_ref[...])) + 0.5
        begin += rows


def project(parts, weights):
    cols, channels = parts[0].shape[1:]
    rows = sum(part.shape[0] for part in parts)
    vmem = pl.BlockSpec(memory_space=pltpu.VMEM)
    sizes = ((cols, LANES), (LANES, cols), (LANES, 2 * LANES), (LANES, 2 * LANES))
    kinds = (jnp.bfloat16,) * 3 + (jnp.float32,)
    return pl.pallas_call(
        functools.partial(project_kernel, len(parts)),
        in_specs=[vmem] * (len(parts) + len(weights)),
        out_specs=[vmem] * 4,
        out_shape=[jax.ShapeDtypeStruct((rows,) + size, kind) for size, kind in zip(sizes, kinds)],
        compiler_params=pltpu.CompilerParams(vmem_limit_bytes=VMEM),
        cost_estimate=pl.CostEstimate(flops=1, bytes_accessed=10, transcendentals=0),
        name="project_own",
    )(*parts, *weights)


def widen_kernel(other_ref, wk_ref, wv_ref, k_ref, v_ref):
    rows, cols, channels = other_ref.shape
    keys = dot(other_ref[...].reshape(rows * cols, channels), wk_ref[...])
    k_ref[...] = keys.astype(jnp.bfloat16).reshape(rows, cols, LANES)
    for row in range(rows):
        v_ref[row] = dot(wv_ref[...], other_ref[row], NT).astype(jnp.bfloat16)


def widen(other, wk, wv):
    rows, cols, _ = other.shape
    vmem = pl.BlockSpec(memory_space=pltpu.VMEM)
    return pl.pallas_call(
        widen_kernel,
        in_specs=[vmem] * 3,
        out_specs=[vmem] * 2,
        out_shape=[
            jax.ShapeDtypeStruct((rows, cols, LANES), jnp.bfloat16),
            jax.ShapeDtypeStruct((rows, LANES, cols), jnp.bfloat16),
        ],
        compiler_params=pltpu.CompilerParams(vmem_limit_bytes=VMEM),
        cost_estimate=pl.CostEstimate(flops=10**10, bytes_accessed=10, transcendentals=0),
        name="widen_rows",
    )(other, wk, wv)


TILE_ROWS = ((0, 32), (32, 64), (0, 64), (64, 96), (96, 128), (64, 128))


def attend_kernel(begin, first, *refs):
    if first:
        k_other, v_other, *refs = refs
    else:
        _, other_ref, wk_ref, wv_ref, *refs = refs
    k_ref, v_ref, q_ref, g_ref, bias_ref, wo_ref, ob_ref, out_ref, v_both, *scratch = refs
    if not first:
        k_other, *scratch = scratch
    scores, weights, tops, shares = (scratch[2 * n : 2 * n + 2] for n in range(4))
    rows, cols, _ = k_other.shape
    keys = 2 * cols
    low = lax.broadcasted_iota(jnp.int32, (32, LANES), 1) < 64
    lanes = [slice(tile * LANES, (tile + 1) * LANES) for tile in range(6)]

    def blank(count):
        return jnp.zeros((count, LANES), jnp.bfloat16)

    def query_tile(row, tile):
        head, tail = TILE_ROWS[tile]
        if tile % 3 < 2:
            part = q_ref[begin + row, head:tail, :LANES]
        else:
            one = q_ref[begin + row, head : head + 32, LANES:]
            two = q_ref[begin + row, head + 32 : tail, LANES:]
            part = jnp.concatenate(
                (jnp.where(low, one, 0), jnp.where(low, 0, two)), 0
            ).astype(jnp.bfloat16)
        pieces = [part]
        if head:
            pieces.insert(0, blank(head))
        if tail < LANES:
            pieces.append(blank(LANES - tail))
        return jnp.concatenate(pieces, 0)

    def widen(row):
        if first:
            values = v_other[row]
        else:
            other = other_ref[row]
            k_other[row] = dot(other, wk_ref[...]).astype(jnp.bfloat16)
            yield
            values = dot(wv_ref[...], other, NT).astype(jnp.bfloat16)
        v_both[row] = jnp.concatenate((v_ref[begin + row], values), 1)
        yield

    def score(row, slot, shift):
        for tile in range(6):
            query = query_tile(row, tile)
            both = jnp.concatenate((k_ref[begin + row], k_other[row]), 0)
            part = dot(both, query) + bias_ref[:keys, lanes[tile]]
            if shift:
                part = part + MISSING
            scores[slot][:, lanes[tile]] = part
            tops[slot][0:1, lanes[tile]] = jnp.max(part, axis=0, keepdims=True)
            yield

    def soften(slot):
        for tile in range(6):
            part = jnp.exp(scores[slot][:, lanes[tile]] - tops[slot][0:1, lanes[tile]])
            shares[slot][0:1, lanes[tile]] = 1.0 / jnp.sum(part, axis=0, keepdims=True)
            weights[slot][:, lanes[tile]] = part.astype(jnp.bfloat16)
            yield

    def mix(row, slot):
        mixed = []
        for tile in range(6):
            head, tail = TILE_ROWS[tile]
            part = dot(v_both[row, head:tail], weights[slot][:, lanes[tile]])
            mixed.append(part * shares[slot][0:1, lanes[tile]])
            yield
        gated = []
        for pair in range(2):
            one, two, both = mixed[3 * pair : 3 * pair + 3]
            gate = g_ref[begin + row, 64 * pair : 64 * pair + 32]
            rest = jnp.where(low, both[:32] * gate[:, LANES:], 0.0)
            gated.append(jnp.concatenate((one * gate[:, :LANES], rest), 1))
            gate = g_ref[begin + row, 64 * pair + 32 : 64 * pair + 64]
            rest = jnp.where(low, 0.0, both[32:] * gate[:, LANES:])
            gated.append(jnp.concatenate((two * gate[:, :LANES], rest), 1))
        update = dot(jnp.concatenate(gated, 0).astype(jnp.bfloat16), wo_ref[...], TN)
        rest = cols - LANES
        update = jnp.concatenate(
            (update[:LANES], update[LANES : LANES + rest] + update[LANES + rest :]), 0
        )
        out_ref[row] = (update + ob_ref[...]).astype(jnp.bfloat16)
        yield

    def run(*stages):
        stages = list(stages)
        while stages:
            stages = [stage for stage in stages if next(stage, True) is None]

    present = bias_ref[keys, 0]

    @pl.when(present > 0.5)
    def _():
        run(widen(0))
        for step in range(rows + 2):
            stages = []
            if step >= 2:
                stages.append(mix(step - 2, step % 2))
            if 1 <= step <= rows:
                stages.append(soften((step - 1) % 2))
            if step < rows:
                stages.append(score(step, step % 2, False))
            if step + 1 < rows:
                stages.append(widen(step + 1))
            run(*stages)

    @pl.when(present <= 0.5)
    def _():
        def one(row, carry):
            run(widen(row))
            run(score(row, 0, True))
            run(soften(0))
            run(mix(row, 0))
            return carry

        lax.fori_loop(0, rows, one, 0)


def attend(head, k, v, q, g, bias, wo, ob, rows, begin):
    total, cols, _ = k.shape
    keys, lanes = 2 * cols, bias.shape[1]
    first = len(head) == 2
    vmem = pl.BlockSpec(memory_space=pltpu.VMEM)
    specs = [vmem] * 2 if first else [pl.BlockSpec(memory_space=pl.ANY)] + [vmem] * 3
    own_keys = [] if first else [pltpu.VMEM((rows, cols, LANES), jnp.bfloat16)]
    return pl.pallas_call(
        functools.partial(attend_kernel, begin, first),
        grid=(1,),
        in_specs=specs + [vmem] * 7,
        out_specs=pl.BlockSpec((rows, cols, LANES), lambda i: (begin // rows, 0, 0)),
        out_shape=jax.ShapeDtypeStruct((total, cols, LANES), jnp.bfloat16),
        scratch_shapes=[pltpu.VMEM((rows, LANES, keys), jnp.bfloat16)]
        + own_keys
        + [pltpu.VMEM((keys, lanes), jnp.float32)] * 2
        + [pltpu.VMEM((keys, lanes), jnp.bfloat16)] * 2
        + [pltpu.VMEM((8, lanes), jnp.float32)] * 4,
        input_output_aliases={} if first else {0: 0},
        compiler_params=pltpu.CompilerParams(vmem_limit_bytes=24 << 20),
        cost_estimate=pl.CostEstimate(flops=10**10, bytes_accessed=10, transcendentals=0),
        name="attend_rows",
    )(*head, k, v, q, g, bias, wo, ob)


def device(z_hi, z_lo, y, core, x):
    return (((z_hi * 2 + z_lo) * 2 + y) * 2 + core) * 2 + x


def moved(array, move):
    pairs = []
    for number in range(32):
        a, b, y, c, x = ((number >> bit) & 1 for bit in (4, 3, 2, 1, 0))
        target = move(a, b, y, c, x)
        if target is not None:
            pairs.append((number, device(*target)))
    return lax.ppermute(array, ("rows", "cols"), pairs)


def spread_tiles(tile, z_hi, x, part):
    straight = moved(tile, lambda a, b, y, c, x: (1 - a, b, y, c, x) if a == x else (a, b, y, c, 1 - x))
    across = moved(tile, lambda a, b, y, c, x: None if a == x else (1 - a, b, y, c, 1 - x))
    straight, part = lax.optimization_barrier((straight, part))
    home = z_hi == x
    pair = jnp.stack((jnp.where(home, tile, straight), jnp.where(home, straight, across)))
    near = [pair]
    for move in (
        lambda a, b, y, c, x: (a, b, 1 - y, c, x),
        lambda a, b, y, c, x: (a, 1 - b, y, c, x),
        lambda a, b, y, c, x: (a, 1 - b, 1 - y, c, x),
    ):
        near.append(moved(pair, move))
    return jnp.concatenate(near, 0), part


def shards_general(
    pair, token_mask, norm_gain, norm_shift, in_weight, gate_bias, bias_weight, out_weight, out_bias
):
    row_count, col_count, channels = pair.shape
    head_count = bias_weight.shape[1]
    inner_width = out_weight.shape[0]
    head_size = inner_width // head_count
    normed = layer_norm(pair, norm_gain, norm_shift)
    flat_normed = normed.reshape(row_count * col_count, channels)
    bias_tile = jnp.einsum(
        "jkc,ch->jhk", normed, bias_weight, preferred_element_type=jnp.float32
    ).astype(jnp.bfloat16)
    bias_columns = lax.all_gather(bias_tile, "rows", axis=0, tiled=True)
    own_bias = lax.all_to_all(bias_columns, "cols", split_axis=0, concat_axis=2, tiled=True)
    query_gate = jnp.concatenate(
        (in_weight[:, :inner_width], in_weight[:, 3 * inner_width :]), axis=1
    )
    projected = jnp.dot(flat_normed, query_gate, preferred_element_type=jnp.float32)
    queries = (projected[:, :inner_width] * head_size ** (-0.5)).astype(jnp.bfloat16)
    queries = queries.reshape(row_count, col_count, head_count, head_size)
    gates = jax.nn.sigmoid(projected[:, inner_width:] + gate_bias)
    key_value_weight = in_weight[:, inner_width : 3 * inner_width]
    mask_row = token_mask.reshape(1, col_count)
    start_state = (
        jnp.full((row_count, col_count, head_count), -jnp.inf, jnp.float32),
        jnp.zeros((row_count, col_count, head_count), jnp.float32),
        jnp.zeros((row_count, col_count, inner_width), jnp.float32),
    )
    key_values = jnp.dot(flat_normed, key_value_weight, preferred_element_type=jnp.float32).astype(
        jnp.bfloat16
    )
    key_values = key_values.reshape(row_count, col_count, 2 * inner_width)
    pair_keys = lax.all_gather(key_values, "cols", axis=1, tiled=True)
    mask_in = lax.all_gather(mask_row, "cols", axis=1, tiled=True)
    state_now = start_state
    begin_at = jnp.int32(0)
    span_len = pair_keys.shape[1]
    for low_edge in range(0, span_len, col_count):
        high_edge = min(low_edge + col_count, span_len)
        attend_pair_keys = pair_keys[:, low_edge:high_edge]
        attend_begin_at = begin_at + low_edge
        attend_running_max, attend_totals, attend_summed = state_now
        attend_span_len = attend_pair_keys.shape[1]
        key_part = attend_pair_keys[..., :inner_width].reshape(
            row_count, attend_span_len, head_count, head_size
        )
        value_part = attend_pair_keys[..., inner_width:].reshape(
            row_count, attend_span_len, head_count, head_size
        )
        scores = jnp.einsum(
            "rjhd,rkhd->rjhk", queries, key_part, preferred_element_type=jnp.float32
        )
        bias_part = lax.dynamic_slice_in_dim(own_bias, attend_begin_at, attend_span_len, 2).astype(
            jnp.float32
        )
        masking = 1000000000.0 * (mask_in[:, low_edge:high_edge][0].astype(jnp.float32) - 1.0)
        scores = scores + bias_part + masking
        new_max = jnp.maximum(attend_running_max, jnp.max(scores, axis=-1))
        shrink = jnp.exp(attend_running_max - new_max)
        weights = jnp.exp(scores - new_max[..., None])
        attend_totals = attend_totals * shrink + jnp.sum(weights, axis=-1)
        mixed_part = jnp.einsum(
            "rjhk,rkhd->rjhd",
            weights.astype(jnp.bfloat16),
            value_part,
            preferred_element_type=jnp.float32,
        )
        attend_summed = (
            attend_summed.reshape(row_count, col_count, head_count, head_size) * shrink[..., None]
            + mixed_part
        )
        state_now = (
            new_max,
            attend_totals,
            attend_summed.reshape(row_count, col_count, inner_width),
        )
    running_max, totals, summed = state_now
    attended = summed.reshape(row_count, col_count, head_count, head_size) / totals[..., None]
    gated = gates.reshape(row_count, col_count, head_count, head_size) * attended
    gated = gated.astype(jnp.bfloat16).reshape(row_count * col_count, inner_width)
    updated = jnp.dot(gated, out_weight, preferred_element_type=jnp.float32) + out_bias
    return updated.astype(jnp.bfloat16).reshape(row_count, col_count, channels)


def fits(mesh, pair_shape, heads, inner):
    rows, cols, channels = pair_shape
    return (
        (mesh.shape["rows"], mesh.shape["cols"]) == (16, 2)
        and (rows, cols, channels) == (24, 192, LANES)
        and (heads, inner) == (4, LANES)
    )


def shards(
    pair, token_mask, norm_gain, norm_shift, in_weight, gate_bias, bias_weight, out_weight, out_bias
):
    rows, cols, channels = pair.shape
    inner = out_weight.shape[0]
    gain, shift = norm_gain.reshape(1, channels), norm_shift.reshape(1, channels)
    swap = [(0, 1), (1, 0)]
    *normed, tile = norm_and_tile(pair, gain, shift, bias_weight, token_mask, CHUNKS)
    wk, wv = in_weight[:, inner : 2 * inner], in_weight[:, 2 * inner : 3 * inner].T
    wqg = jnp.concatenate((in_weight[:, :inner].T, in_weight[:, 3 * inner :].T), 0)
    own = list(project(normed, (wk, wv, wqg, gate_bias.reshape(inner, 1))))
    row = lax.axis_index("rows")
    x = lax.axis_index("cols")
    z_hi, z_lo, y, core = row >> 3, (row >> 2) & 1, (row >> 1) & 1, row & 1
    near, normed[1] = spread_tiles(tile, z_hi, x, normed[1])
    near, *own = lax.optimization_barrier((near, *own))
    others = [lax.ppermute(part, "cols", swap) for part in normed[:2]]
    head = list(widen(others[0], wk, wv))
    normed[2], head[0] = lax.optimization_barrier((normed[2], head[0]))
    others.append(lax.ppermute(normed[2], "cols", swap))
    far = moved(near, lambda a, b, y, c, x: (a, b, y, 1 - c, x))
    place = jnp.arange(16, dtype=jnp.int32)
    half, a, b, c = place >> 3, (place >> 2) & 1, (place >> 1) & 1, place & 1
    index = (c ^ core) * 8 + (a ^ z_lo) * 4 + (b ^ y) * 2 + half
    bias = assemble(index, near, far, lane_order(cols, rows, 8))
    tail = (*own, bias, out_weight, out_bias.reshape(1, channels))
    out = attend(head, *tail, CHUNKS[0][1], CHUNKS[0][0])
    for (begin, count), other in zip(CHUNKS[1:], others[1:]):
        other, out = lax.optimization_barrier((other, out))
        out = attend((out, other, wk, wv), *tail, count, begin)
    return out


def solution(mesh):
    placed = (P("rows", "cols", None), P("cols"), P(), P(), P(), P(), P(), P(), P())

    def run(pair, *rest):
        tall, wide, channels = pair.shape
        block = (tall // mesh.shape["rows"], wide // mesh.shape["cols"], channels)
        bias_weight, out_weight = rest[5], rest[6]
        special = fits(mesh, block, bias_weight.shape[1], out_weight.shape[0])
        return jax.shard_map(
            shards if special else shards_general,
            mesh=mesh,
            in_specs=placed,
            out_specs=P("rows", "cols", None),
            check_vma=False,
        )(pair, *rest)

    return run
```

```python
import functools

import jax
import jax.numpy as jnp
import numpy as np
from jax import lax
from jax.experimental import pallas as pl
from jax.experimental.pallas import tpu as pltpu
from jax.sharding import PartitionSpec as P

LANES = 128
MISSING = -1e9
NN = (((1,), (0,)), ((), ()))
NT = (((1,), (1,)), ((), ()))
TN = (((0,), (0,)), ((), ()))
CHUNKS = ((0, 8), (8, 8), (16, 8))
VMEM = 14 << 20
ALL_VMEM = 60 << 20


def dot(left, right, dims=NN):
    return lax.dot_general(left, right, dims, preferred_element_type=jnp.float32)


def layer_norm(pair_block, norm_gain, norm_shift):
    as_float = pair_block.astype(jnp.float32)
    center = jnp.mean(as_float, axis=-1, keepdims=True)
    spread = jnp.mean(jnp.square(as_float - center), axis=-1, keepdims=True)
    return ((as_float - center) * lax.rsqrt(spread + 1e-05) * norm_gain + norm_shift).astype(
        jnp.bfloat16
    )


def normed_rows(block, mean_weight, gain, shift):
    center = block.astype(jnp.float32) - dot(block, mean_weight)
    spread = jnp.mean(center * center, axis=-1, keepdims=True)
    return (center * lax.rsqrt(spread + 1e-05) * gain + shift).astype(jnp.bfloat16)


def norm_kernel(parts, pair_hbm, *refs):
    small_hbm, refs = refs[:4], refs[4:]
    normed_refs, tile_ref, refs = refs[: len(parts)], refs[len(parts)], refs[len(parts) + 1 :]
    pair_ref, gain_ref, shift_ref, weight_ref, mask_ref, done = refs
    rows, slots = pair_ref.shape[0], 32
    copies = [
        pltpu.make_async_copy(source, target, done.at[place])
        for place, (source, target) in enumerate(
            zip(small_hbm, (gain_ref, shift_ref, weight_ref, mask_ref))
        )
    ]
    for place, (begin, count) in enumerate(parts):
        block = pl.ds(begin, count)
        copies.append(
            pltpu.make_async_copy(pair_hbm.at[block], pair_ref.at[block], done.at[4 + place])
        )
    for copy in copies:
        copy.start()
    for copy in copies[:4]:
        copy.wait()

    heads = weight_ref.shape[0]
    head = lax.broadcasted_iota(jnp.int32, (heads, LANES), 0)
    place = lax.broadcasted_iota(jnp.int32, (heads, LANES), 1)
    expand = jnp.logical_and(place >= head * slots, place < head * slots + slots)
    wide = dot(weight_ref[...], expand.astype(jnp.bfloat16), TN)
    spot = lax.broadcasted_iota(jnp.int32, (1, LANES), 1) == rows
    total = dot(mask_ref[...].astype(jnp.bfloat16), spot.astype(jnp.bfloat16), TN)
    slot = lax.rem(lax.broadcasted_iota(jnp.int32, (LANES, LANES), 1), slots)
    mean_weight = jnp.full((LANES, LANES), 1 / LANES, jnp.bfloat16)
    for (begin, count), copy, normed_ref in zip(parts, copies[4:], normed_refs):
        copy.wait()
        left, right = [], []
        for row in range(begin, begin + count):
            normed = normed_rows(pair_ref[row], mean_weight, gain_ref[...], shift_ref[...])
            normed_ref[row - begin] = normed
            left.append(normed)
            right.append(jnp.where(slot == row, wide, 0.0).astype(jnp.bfloat16))
        total += dot(jnp.concatenate(left, 1), jnp.concatenate(right, 0))
    tile_ref[...] = total.astype(jnp.bfloat16)


def norm_and_tile(pair, gain, shift, bias_weight, mask, parts):
    rows, cols, channels = pair.shape
    small = (gain, shift, bias_weight.T, mask.reshape(1, cols))
    vmem = pl.BlockSpec(memory_space=pltpu.VMEM)
    return pl.pallas_call(
        functools.partial(norm_kernel, parts),
        in_specs=[pl.BlockSpec(memory_space=pltpu.HBM)] * 5,
        out_specs=[vmem] * (len(parts) + 1),
        out_shape=[
            jax.ShapeDtypeStruct((count, cols, channels), jnp.bfloat16) for _, count in parts
        ]
        + [jax.ShapeDtypeStruct((cols, LANES), jnp.bfloat16)],
        scratch_shapes=[pltpu.VMEM(pair.shape, pair.dtype)]
        + [pltpu.VMEM(a.shape, a.dtype) for a in small]
        + [pltpu.SemaphoreType.DMA((4 + len(parts),))],
        compiler_params=pltpu.CompilerParams(vmem_limit_bytes=ALL_VMEM),
        cost_estimate=pl.CostEstimate(flops=10**9, bytes_accessed=10**7, transcendentals=0),
        name="norm_and_tile",
    )(pair, *small)


def assemble_kernel(index_ref, near_ref, far_ref, order_ref, bias_ref, tiles, marks):
    count, cols, _ = near_ref.shape
    tiles[:count] = near_ref[...]
    tiles[count:] = far_ref[...]
    for half in range(2):
        taken = [tiles[index_ref[half * count + place]] for place in range(count)]
        marks[half * cols : (half + 1) * cols] = taken[0].astype(jnp.float32)[:, 24:25]
        bias_ref[half * cols : (half + 1) * cols] = dot(
            jnp.concatenate(taken, 1), order_ref[...]
        )
    present = jnp.max(marks[...], axis=0, keepdims=True)
    hidden = jnp.logical_and(marks[...] < 0.5, present > 0.5)
    bias_ref[: 2 * cols] = jnp.where(hidden, MISSING, bias_ref[: 2 * cols])
    bias_ref[2 * cols :] = jnp.broadcast_to(present, (8, bias_ref.shape[1]))


def lane_order(cols, rows, places):
    order = np.zeros((places * LANES, 4 * cols), np.float32)
    for place in range(places):
        for head in range(4):
            for row in range(rows):
                query = place * rows + row
                base = (head // 2) * 2 * cols
                if query < LANES:
                    lane = base + (head % 2) * LANES + query
                else:
                    lane = base + 2 * LANES + (head % 2) * (cols - LANES) + query - LANES
                order[place * LANES + head * 32 + row, lane] = 1
    return jnp.asarray(order, jnp.bfloat16)


def assemble(index, near, far, order):
    count, cols, _ = near.shape
    vmem = pl.BlockSpec(memory_space=pltpu.VMEM)
    smem = pl.BlockSpec(memory_space=pltpu.SMEM)
    return pl.pallas_call(
        assemble_kernel,
        in_specs=[smem, vmem, vmem, vmem],
        out_specs=vmem,
        out_shape=jax.ShapeDtypeStruct((2 * cols + 8, order.shape[1]), jnp.float32),
        scratch_shapes=[
            pltpu.VMEM((2 * count, cols, LANES), jnp.bfloat16),
            pltpu.VMEM((2 * cols, 1), jnp.float32),
        ],
        compiler_params=pltpu.CompilerParams(vmem_limit_bytes=VMEM),
        cost_estimate=pl.CostEstimate(flops=10**9, bytes_accessed=4 * 10**6, transcendentals=0),
        name="assemble_bias",
    )(index, near, far, order)


def project_kernel(count, *refs):
    own_refs, refs = refs[:count], refs[count:]
    wk_ref, wv_ref, wqg_ref, gb_ref, k_ref, v_ref, q_ref, g_ref = refs
    begin = 0
    for own_ref in own_refs:
        rows, cols, channels = own_ref.shape
        keys = dot(own_ref[...].reshape(rows * cols, channels), wk_ref[...])
        k_ref[begin : begin + rows] = keys.astype(jnp.bfloat16).reshape(rows, cols, LANES)
        for row in range(rows):
            own = own_ref[row]
            v_ref[begin + row] = dot(wv_ref[...], own, NT).astype(jnp.bfloat16)
            mixed = dot(wqg_ref[...], jnp.concatenate((own, own[LANES:]), 0), NT)
            q_ref[begin + row] = (mixed[:LANES] * 32 ** (-0.5)).astype(jnp.bfloat16)
            g_ref[begin + row] = 0.5 * jnp.tanh(0.5 * (mixed[LANES:] + gb_ref[...])) + 0.5
        begin += rows


def project(parts, weights):
    cols, channels = parts[0].shape[1:]
    rows = sum(part.shape[0] for part in parts)
    vmem = pl.BlockSpec(memory_space=pltpu.VMEM)
    sizes = ((cols, LANES), (LANES, cols), (LANES, 2 * LANES), (LANES, 2 * LANES))
    kinds = (jnp.bfloat16,) * 3 + (jnp.float32,)
    return pl.pallas_call(
        functools.partial(project_kernel, len(parts)),
        in_specs=[vmem] * (len(parts) + len(weights)),
        out_specs=[vmem] * 4,
        out_shape=[jax.ShapeDtypeStruct((rows,) + size, kind) for size, kind in zip(sizes, kinds)],
        compiler_params=pltpu.CompilerParams(vmem_limit_bytes=VMEM),
        cost_estimate=pl.CostEstimate(flops=1, bytes_accessed=10, transcendentals=0),
        name="project_own",
    )(*parts, *weights)


def widen_kernel(other_ref, wk_ref, wv_ref, k_ref, v_ref):
    rows, cols, channels = other_ref.shape
    keys = dot(other_ref[...].reshape(rows * cols, channels), wk_ref[...])
    k_ref[...] = keys.astype(jnp.bfloat16).reshape(rows, cols, LANES)
    for row in range(rows):
        v_ref[row] = dot(wv_ref[...], other_ref[row], NT).astype(jnp.bfloat16)


def widen(other, wk, wv):
    rows, cols, _ = other.shape
    vmem = pl.BlockSpec(memory_space=pltpu.VMEM)
    return pl.pallas_call(
        widen_kernel,
        in_specs=[vmem] * 3,
        out_specs=[vmem] * 2,
        out_shape=[
            jax.ShapeDtypeStruct((rows, cols, LANES), jnp.bfloat16),
            jax.ShapeDtypeStruct((rows, LANES, cols), jnp.bfloat16),
        ],
        compiler_params=pltpu.CompilerParams(vmem_limit_bytes=VMEM),
        cost_estimate=pl.CostEstimate(flops=10**10, bytes_accessed=10, transcendentals=0),
        name="widen_rows",
    )(other, wk, wv)


TILE_ROWS = ((0, 32), (32, 64), (0, 64), (64, 96), (96, 128), (64, 128))


def attend_kernel(begin, first, *refs):
    if first:
        k_other, v_other, *refs = refs
    else:
        _, other_ref, wk_ref, wv_ref, *refs = refs
    k_ref, v_ref, q_ref, g_ref, bias_ref, wo_ref, ob_ref, out_ref, v_both, *scratch = refs
    if not first:
        k_other, *scratch = scratch
    scores, weights, tops, shares = (scratch[2 * n : 2 * n + 2] for n in range(4))
    rows, cols, _ = k_other.shape
    keys = 2 * cols
    low = lax.broadcasted_iota(jnp.int32, (32, LANES), 1) < 64
    lanes = [slice(tile * LANES, (tile + 1) * LANES) for tile in range(6)]

    def blank(count):
        return jnp.zeros((count, LANES), jnp.bfloat16)

    def query_tile(row, tile):
        head, tail = TILE_ROWS[tile]
        if tile % 3 < 2:
            part = q_ref[begin + row, head:tail, :LANES]
        else:
            one = q_ref[begin + row, head : head + 32, LANES:]
            two = q_ref[begin + row, head + 32 : tail, LANES:]
            part = jnp.concatenate(
                (jnp.where(low, one, 0), jnp.where(low, 0, two)), 0
            ).astype(jnp.bfloat16)
        pieces = [part]
        if head:
            pieces.insert(0, blank(head))
        if tail < LANES:
            pieces.append(blank(LANES - tail))
        return jnp.concatenate(pieces, 0)

    def widen(row):
        if first:
            values = v_other[row]
        else:
            other = other_ref[row]
            k_other[row] = dot(other, wk_ref[...]).astype(jnp.bfloat16)
            yield
            values = dot(wv_ref[...], other, NT).astype(jnp.bfloat16)
        v_both[row] = jnp.concatenate((v_ref[begin + row], values), 1)
        yield

    def score(row, slot, shift):
        for tile in range(6):
            query = query_tile(row, tile)
            both = jnp.concatenate((k_ref[begin + row], k_other[row]), 0)
            part = dot(both, query) + bias_ref[:keys, lanes[tile]]
            if shift:
                part = part + MISSING
            scores[slot][:, lanes[tile]] = part
            tops[slot][0:1, lanes[tile]] = jnp.max(part, axis=0, keepdims=True)
            yield

    def soften(slot):
        for tile in range(6):
            part = jnp.exp(scores[slot][:, lanes[tile]] - tops[slot][0:1, lanes[tile]])
            shares[slot][0:1, lanes[tile]] = 1.0 / jnp.sum(part, axis=0, keepdims=True)
            weights[slot][:, lanes[tile]] = part.astype(jnp.bfloat16)
            yield

    def mix(row, slot):
        mixed = []
        for tile in range(6):
            head, tail = TILE_ROWS[tile]
            part = dot(v_both[row, head:tail], weights[slot][:, lanes[tile]])
            mixed.append(part * shares[slot][0:1, lanes[tile]])
            yield
        gated = []
        for pair in range(2):
            one, two, both = mixed[3 * pair : 3 * pair + 3]
            gate = g_ref[begin + row, 64 * pair : 64 * pair + 32]
            rest = jnp.where(low, both[:32] * gate[:, LANES:], 0.0)
            gated.append(jnp.concatenate((one * gate[:, :LANES], rest), 1))
            gate = g_ref[begin + row, 64 * pair + 32 : 64 * pair + 64]
            rest = jnp.where(low, 0.0, both[32:] * gate[:, LANES:])
            gated.append(jnp.concatenate((two * gate[:, :LANES], rest), 1))
        update = dot(jnp.concatenate(gated, 0).astype(jnp.bfloat16), wo_ref[...], TN)
        rest = cols - LANES
        update = jnp.concatenate(
            (update[:LANES], update[LANES : LANES + rest] + update[LANES + rest :]), 0
        )
        out_ref[row] = (update + ob_ref[...]).astype(jnp.bfloat16)
        yield

    def run(*stages):
        stages = list(stages)
        while stages:
            stages = [stage for stage in stages if next(stage, True) is None]

    present = bias_ref[keys, 0]

    @pl.when(present > 0.5)
    def _():
        run(widen(0))
        for step in range(rows + 2):
            stages = []
            if step >= 2:
                stages.append(mix(step - 2, step % 2))
            if 1 <= step <= rows:
                stages.append(soften((step - 1) % 2))
            if step < rows:
                stages.append(score(step, step % 2, False))
            if step + 1 < rows:
                stages.append(widen(step + 1))
            run(*stages)

    @pl.when(present <= 0.5)
    def _():
        def one(row, carry):
            run(widen(row))
            run(score(row, 0, True))
            run(soften(0))
            run(mix(row, 0))
            return carry

        lax.fori_loop(0, rows, one, 0)


def attend(head, k, v, q, g, bias, wo, ob, rows, begin):
    total, cols, _ = k.shape
    keys, lanes = 2 * cols, bias.shape[1]
    first = len(head) == 2
    vmem = pl.BlockSpec(memory_space=pltpu.VMEM)
    specs = [vmem] * 2 if first else [pl.BlockSpec(memory_space=pl.ANY)] + [vmem] * 3
    own_keys = [] if first else [pltpu.VMEM((rows, cols, LANES), jnp.bfloat16)]
    return pl.pallas_call(
        functools.partial(attend_kernel, begin, first),
        grid=(1,),
        in_specs=specs + [vmem] * 7,
        out_specs=pl.BlockSpec((rows, cols, LANES), lambda i: (begin // rows, 0, 0)),
        out_shape=jax.ShapeDtypeStruct((total, cols, LANES), jnp.bfloat16),
        scratch_shapes=[pltpu.VMEM((rows, LANES, keys), jnp.bfloat16)]
        + own_keys
        + [pltpu.VMEM((keys, lanes), jnp.float32)] * 2
        + [pltpu.VMEM((keys, lanes), jnp.bfloat16)] * 2
        + [pltpu.VMEM((8, lanes), jnp.float32)] * 4,
        input_output_aliases={} if first else {0: 0},
        compiler_params=pltpu.CompilerParams(vmem_limit_bytes=24 << 20),
        cost_estimate=pl.CostEstimate(flops=10**10, bytes_accessed=10, transcendentals=0),
        name="attend_rows",
    )(*head, k, v, q, g, bias, wo, ob)


def device(z_hi, z_lo, y, core, x):
    return (((z_hi * 2 + z_lo) * 2 + y) * 2 + core) * 2 + x


def moved(array, move):
    pairs = []
    for number in range(32):
        a, b, y, c, x = ((number >> bit) & 1 for bit in (4, 3, 2, 1, 0))
        target = move(a, b, y, c, x)
        if target is not None:
            pairs.append((number, device(*target)))
    return lax.ppermute(array, ("rows", "cols"), pairs)


def spread_tiles(tile, z_hi, x, part):
    across = moved(tile, lambda a, b, y, c, x: None if a == x else (1 - a, b, y, c, 1 - x))
    straight = moved(tile, lambda a, b, y, c, x: (1 - a, b, y, c, x) if a == x else (a, b, y, c, 1 - x))
    across, part = lax.optimization_barrier((across, part))
    home = z_hi == x
    pair = jnp.stack((jnp.where(home, tile, straight), jnp.where(home, straight, across)))
    near = [pair]
    for move in (
        lambda a, b, y, c, x: (a, b, 1 - y, c, x),
        lambda a, b, y, c, x: (a, 1 - b, y, c, x),
        lambda a, b, y, c, x: (a, 1 - b, 1 - y, c, x),
    ):
        near.append(moved(pair, move))
    return jnp.concatenate(near, 0), part


def shards_general(
    pair, token_mask, norm_gain, norm_shift, in_weight, gate_bias, bias_weight, out_weight, out_bias
):
    row_count, col_count, channels = pair.shape
    head_count = bias_weight.shape[1]
    inner_width = out_weight.shape[0]
    head_size = inner_width // head_count
    normed = layer_norm(pair, norm_gain, norm_shift)
    flat_normed = normed.reshape(row_count * col_count, channels)
    bias_tile = jnp.einsum(
        "jkc,ch->jhk", normed, bias_weight, preferred_element_type=jnp.float32
    ).astype(jnp.bfloat16)
    bias_columns = lax.all_gather(bias_tile, "rows", axis=0, tiled=True)
    own_bias = lax.all_to_all(bias_columns, "cols", split_axis=0, concat_axis=2, tiled=True)
    query_gate = jnp.concatenate(
        (in_weight[:, :inner_width], in_weight[:, 3 * inner_width :]), axis=1
    )
    projected = jnp.dot(flat_normed, query_gate, preferred_element_type=jnp.float32)
    queries = (projected[:, :inner_width] * head_size ** (-0.5)).astype(jnp.bfloat16)
    queries = queries.reshape(row_count, col_count, head_count, head_size)
    gates = jax.nn.sigmoid(projected[:, inner_width:] + gate_bias)
    key_value_weight = in_weight[:, inner_width : 3 * inner_width]
    mask_row = token_mask.reshape(1, col_count)
    start_state = (
        jnp.full((row_count, col_count, head_count), -jnp.inf, jnp.float32),
        jnp.zeros((row_count, col_count, head_count), jnp.float32),
        jnp.zeros((row_count, col_count, inner_width), jnp.float32),
    )
    key_values = jnp.dot(flat_normed, key_value_weight, preferred_element_type=jnp.float32).astype(
        jnp.bfloat16
    )
    key_values = key_values.reshape(row_count, col_count, 2 * inner_width)
    pair_keys = lax.all_gather(key_values, "cols", axis=1, tiled=True)
    mask_in = lax.all_gather(mask_row, "cols", axis=1, tiled=True)
    state_now = start_state
    begin_at = jnp.int32(0)
    span_len = pair_keys.shape[1]
    for low_edge in range(0, span_len, col_count):
        high_edge = min(low_edge + col_count, span_len)
        attend_pair_keys = pair_keys[:, low_edge:high_edge]
        attend_begin_at = begin_at + low_edge
        attend_running_max, attend_totals, attend_summed = state_now
        attend_span_len = attend_pair_keys.shape[1]
        key_part = attend_pair_keys[..., :inner_width].reshape(
            row_count, attend_span_len, head_count, head_size
        )
        value_part = attend_pair_keys[..., inner_width:].reshape(
            row_count, attend_span_len, head_count, head_size
        )
        scores = jnp.einsum(
            "rjhd,rkhd->rjhk", queries, key_part, preferred_element_type=jnp.float32
        )
        bias_part = lax.dynamic_slice_in_dim(own_bias, attend_begin_at, attend_span_len, 2).astype(
            jnp.float32
        )
        masking = 1000000000.0 * (mask_in[:, low_edge:high_edge][0].astype(jnp.float32) - 1.0)
        scores = scores + bias_part + masking
        new_max = jnp.maximum(attend_running_max, jnp.max(scores, axis=-1))
        shrink = jnp.exp(attend_running_max - new_max)
        weights = jnp.exp(scores - new_max[..., None])
        attend_totals = attend_totals * shrink + jnp.sum(weights, axis=-1)
        mixed_part = jnp.einsum(
            "rjhk,rkhd->rjhd",
            weights.astype(jnp.bfloat16),
            value_part,
            preferred_element_type=jnp.float32,
        )
        attend_summed = (
            attend_summed.reshape(row_count, col_count, head_count, head_size) * shrink[..., None]
            + mixed_part
        )
        state_now = (
            new_max,
            attend_totals,
            attend_summed.reshape(row_count, col_count, inner_width),
        )
    running_max, totals, summed = state_now
    attended = summed.reshape(row_count, col_count, head_count, head_size) / totals[..., None]
    gated = gates.reshape(row_count, col_count, head_count, head_size) * attended
    gated = gated.astype(jnp.bfloat16).reshape(row_count * col_count, inner_width)
    updated = jnp.dot(gated, out_weight, preferred_element_type=jnp.float32) + out_bias
    return updated.astype(jnp.bfloat16).reshape(row_count, col_count, channels)


def fits(mesh, pair_shape, heads, inner):
    rows, cols, channels = pair_shape
    return (
        (mesh.shape["rows"], mesh.shape["cols"]) == (16, 2)
        and (rows, cols, channels) == (24, 192, LANES)
        and (heads, inner) == (4, LANES)
    )


def shards(
    pair, token_mask, norm_gain, norm_shift, in_weight, gate_bias, bias_weight, out_weight, out_bias
):
    rows, cols, channels = pair.shape
    inner = out_weight.shape[0]
    gain, shift = norm_gain.reshape(1, channels), norm_shift.reshape(1, channels)
    swap = [(0, 1), (1, 0)]
    *normed, tile = norm_and_tile(pair, gain, shift, bias_weight, token_mask, CHUNKS)
    wk, wv = in_weight[:, inner : 2 * inner], in_weight[:, 2 * inner : 3 * inner].T
    wqg = jnp.concatenate((in_weight[:, :inner].T, in_weight[:, 3 * inner :].T), 0)
    own = list(project(normed, (wk, wv, wqg, gate_bias.reshape(inner, 1))))
    row = lax.axis_index("rows")
    x = lax.axis_index("cols")
    z_hi, z_lo, y, core = row >> 3, (row >> 2) & 1, (row >> 1) & 1, row & 1
    near, normed[1] = spread_tiles(tile, z_hi, x, normed[1])
    near, *own = lax.optimization_barrier((near, *own))
    others = [lax.ppermute(part, "cols", swap) for part in normed[:2]]
    head = list(widen(others[0], wk, wv))
    normed[2], head[0] = lax.optimization_barrier((normed[2], head[0]))
    others.append(lax.ppermute(normed[2], "cols", swap))
    far = moved(near, lambda a, b, y, c, x: (a, b, y, 1 - c, x))
    place = jnp.arange(16, dtype=jnp.int32)
    half, a, b, c = place >> 3, (place >> 2) & 1, (place >> 1) & 1, place & 1
    index = (c ^ core) * 8 + (a ^ z_lo) * 4 + (b ^ y) * 2 + half
    bias = assemble(index, near, far, lane_order(cols, rows, 8))
    tail = (*own, bias, out_weight, out_bias.reshape(1, channels))
    out = attend(head, *tail, CHUNKS[0][1], CHUNKS[0][0])
    for (begin, count), other in zip(CHUNKS[1:], others[1:]):
        other, out = lax.optimization_barrier((other, out))
        out = attend((out, other, wk, wv), *tail, count, begin)
    return out


def solution(mesh):
    placed = (P("rows", "cols", None), P("cols"), P(), P(), P(), P(), P(), P(), P())

    def run(pair, *rest):
        tall, wide, channels = pair.shape
        block = (tall // mesh.shape["rows"], wide // mesh.shape["cols"], channels)
        bias_weight, out_weight = rest[5], rest[6]
        special = fits(mesh, block, bias_weight.shape[1], out_weight.shape[0])
        return jax.shard_map(
            shards if special else shards_general,
            mesh=mesh,
            in_specs=placed,
            out_specs=P("rows", "cols", None),
            check_vma=False,
        )(pair, *rest)

    return run
```

```python
import functools

import jax
import jax.numpy as jnp
import numpy as np
from jax import lax
from jax.experimental import pallas as pl
from jax.experimental.pallas import tpu as pltpu
from jax.sharding import PartitionSpec as P

LANES = 128
MISSING = -1e9
NN = (((1,), (0,)), ((), ()))
NT = (((1,), (1,)), ((), ()))
TN = (((0,), (0,)), ((), ()))
CHUNKS = ((0, 8), (8, 8), (16, 8))
VMEM = 14 << 20
ALL_VMEM = 60 << 20


def dot(left, right, dims=NN):
    return lax.dot_general(left, right, dims, preferred_element_type=jnp.float32)


def layer_norm(pair_block, norm_gain, norm_shift):
    as_float = pair_block.astype(jnp.float32)
    center = jnp.mean(as_float, axis=-1, keepdims=True)
    spread = jnp.mean(jnp.square(as_float - center), axis=-1, keepdims=True)
    return ((as_float - center) * lax.rsqrt(spread + 1e-05) * norm_gain + norm_shift).astype(
        jnp.bfloat16
    )


def normed_rows(block, mean_weight, gain, shift):
    center = block.astype(jnp.float32) - dot(block, mean_weight)
    spread = jnp.mean(center * center, axis=-1, keepdims=True)
    return (center * lax.rsqrt(spread + 1e-05) * gain + shift).astype(jnp.bfloat16)


def norm_kernel(parts, pair_hbm, *refs):
    small_hbm, refs = refs[:4], refs[4:]
    normed_refs, tile_ref, refs = refs[: len(parts)], refs[len(parts)], refs[len(parts) + 1 :]
    pair_ref, gain_ref, shift_ref, weight_ref, mask_ref, done = refs
    rows, slots = pair_ref.shape[0], 32
    copies = [
        pltpu.make_async_copy(source, target, done.at[place])
        for place, (source, target) in enumerate(
            zip(small_hbm, (gain_ref, shift_ref, weight_ref, mask_ref))
        )
    ]
    for place, (begin, count) in enumerate(parts):
        block = pl.ds(begin, count)
        copies.append(
            pltpu.make_async_copy(pair_hbm.at[block], pair_ref.at[block], done.at[4 + place])
        )
    for copy in copies:
        copy.start()
    for copy in copies[:4]:
        copy.wait()

    heads = weight_ref.shape[0]
    head = lax.broadcasted_iota(jnp.int32, (heads, LANES), 0)
    place = lax.broadcasted_iota(jnp.int32, (heads, LANES), 1)
    expand = jnp.logical_and(place >= head * slots, place < head * slots + slots)
    wide = dot(weight_ref[...], expand.astype(jnp.bfloat16), TN)
    spot = lax.broadcasted_iota(jnp.int32, (1, LANES), 1) == rows
    total = dot(mask_ref[...].astype(jnp.bfloat16), spot.astype(jnp.bfloat16), TN)
    slot = lax.rem(lax.broadcasted_iota(jnp.int32, (LANES, LANES), 1), slots)
    mean_weight = jnp.full((LANES, LANES), 1 / LANES, jnp.bfloat16)
    for (begin, count), copy, normed_ref in zip(parts, copies[4:], normed_refs):
        copy.wait()
        left, right = [], []
        for row in range(begin, begin + count):
            normed = normed_rows(pair_ref[row], mean_weight, gain_ref[...], shift_ref[...])
            normed_ref[row - begin] = normed
            left.append(normed)
            right.append(jnp.where(slot == row, wide, 0.0).astype(jnp.bfloat16))
        total += dot(jnp.concatenate(left, 1), jnp.concatenate(right, 0))
    tile_ref[...] = total.astype(jnp.bfloat16)


def norm_and_tile(pair, gain, shift, bias_weight, mask, parts):
    rows, cols, channels = pair.shape
    small = (gain, shift, bias_weight.T, mask.reshape(1, cols))
    vmem = pl.BlockSpec(memory_space=pltpu.VMEM)
    return pl.pallas_call(
        functools.partial(norm_kernel, parts),
        in_specs=[pl.BlockSpec(memory_space=pltpu.HBM)] * 5,
        out_specs=[vmem] * (len(parts) + 1),
        out_shape=[
            jax.ShapeDtypeStruct((count, cols, channels), jnp.bfloat16) for _, count in parts
        ]
        + [jax.ShapeDtypeStruct((cols, LANES), jnp.bfloat16)],
        scratch_shapes=[pltpu.VMEM(pair.shape, pair.dtype)]
        + [pltpu.VMEM(a.shape, a.dtype) for a in small]
        + [pltpu.SemaphoreType.DMA((4 + len(parts),))],
        compiler_params=pltpu.CompilerParams(vmem_limit_bytes=ALL_VMEM),
        cost_estimate=pl.CostEstimate(flops=10**9, bytes_accessed=10**7, transcendentals=0),
        name="norm_and_tile",
    )(pair, *small)


def assemble_kernel(index_ref, near_ref, far_ref, order_ref, bias_ref, tiles, marks):
    count, cols, _ = near_ref.shape
    tiles[:count] = near_ref[...]
    tiles[count:] = far_ref[...]
    for half in range(2):
        taken = [tiles[index_ref[half * count + place]] for place in range(count)]
        marks[half * cols : (half + 1) * cols] = taken[0].astype(jnp.float32)[:, 24:25]
        bias_ref[half * cols : (half + 1) * cols] = dot(
            jnp.concatenate(taken, 1), order_ref[...]
        )
    present = jnp.max(marks[...], axis=0, keepdims=True)
    hidden = jnp.logical_and(marks[...] < 0.5, present > 0.5)
    bias_ref[: 2 * cols] = jnp.where(hidden, MISSING, bias_ref[: 2 * cols])
    bias_ref[2 * cols :] = jnp.broadcast_to(present, (8, bias_ref.shape[1]))


def lane_order(cols, rows, places):
    order = np.zeros((places * LANES, 4 * cols), np.float32)
    for place in range(places):
        for head in range(4):
            for row in range(rows):
                query = place * rows + row
                base = (head // 2) * 2 * cols
                if query < LANES:
                    lane = base + (head % 2) * LANES + query
                else:
                    lane = base + 2 * LANES + (head % 2) * (cols - LANES) + query - LANES
                order[place * LANES + head * 32 + row, lane] = 1
    return jnp.asarray(order, jnp.bfloat16)


def assemble(index, near, far, order):
    count, cols, _ = near.shape
    vmem = pl.BlockSpec(memory_space=pltpu.VMEM)
    smem = pl.BlockSpec(memory_space=pltpu.SMEM)
    return pl.pallas_call(
        assemble_kernel,
        in_specs=[smem, vmem, vmem, vmem],
        out_specs=vmem,
        out_shape=jax.ShapeDtypeStruct((2 * cols + 8, order.shape[1]), jnp.float32),
        scratch_shapes=[
            pltpu.VMEM((2 * count, cols, LANES), jnp.bfloat16),
            pltpu.VMEM((2 * cols, 1), jnp.float32),
        ],
        compiler_params=pltpu.CompilerParams(vmem_limit_bytes=VMEM),
        cost_estimate=pl.CostEstimate(flops=10**9, bytes_accessed=4 * 10**6, transcendentals=0),
        name="assemble_bias",
    )(index, near, far, order)


def project_kernel(count, *refs):
    own_refs, refs = refs[:count], refs[count:]
    wk_ref, wv_ref, wqg_ref, gb_ref, k_ref, v_ref, q_ref, g_ref = refs
    begin = 0
    for own_ref in own_refs:
        rows, cols, channels = own_ref.shape
        keys = dot(own_ref[...].reshape(rows * cols, channels), wk_ref[...])
        k_ref[begin : begin + rows] = keys.astype(jnp.bfloat16).reshape(rows, cols, LANES)
        for row in range(rows):
            own = own_ref[row]
            v_ref[begin + row] = dot(wv_ref[...], own, NT).astype(jnp.bfloat16)
            mixed = dot(wqg_ref[...], jnp.concatenate((own, own[LANES:]), 0), NT)
            q_ref[begin + row] = (mixed[:LANES] * 32 ** (-0.5)).astype(jnp.bfloat16)
            g_ref[begin + row] = 0.5 * jnp.tanh(0.5 * (mixed[LANES:] + gb_ref[...])) + 0.5
        begin += rows


def project(parts, weights):
    cols, channels = parts[0].shape[1:]
    rows = sum(part.shape[0] for part in parts)
    vmem = pl.BlockSpec(memory_space=pltpu.VMEM)
    sizes = ((cols, LANES), (LANES, cols), (LANES, 2 * LANES), (LANES, 2 * LANES))
    kinds = (jnp.bfloat16,) * 3 + (jnp.float32,)
    return pl.pallas_call(
        functools.partial(project_kernel, len(parts)),
        in_specs=[vmem] * (len(parts) + len(weights)),
        out_specs=[vmem] * 4,
        out_shape=[jax.ShapeDtypeStruct((rows,) + size, kind) for size, kind in zip(sizes, kinds)],
        compiler_params=pltpu.CompilerParams(vmem_limit_bytes=VMEM),
        cost_estimate=pl.CostEstimate(flops=1, bytes_accessed=10, transcendentals=0),
        name="project_own",
    )(*parts, *weights)


def widen_kernel(other_ref, wk_ref, wv_ref, k_ref, v_ref):
    rows, cols, channels = other_ref.shape
    keys = dot(other_ref[...].reshape(rows * cols, channels), wk_ref[...])
    k_ref[...] = keys.astype(jnp.bfloat16).reshape(rows, cols, LANES)
    for row in range(rows):
        v_ref[row] = dot(wv_ref[...], other_ref[row], NT).astype(jnp.bfloat16)


def widen(other, wk, wv):
    rows, cols, _ = other.shape
    vmem = pl.BlockSpec(memory_space=pltpu.VMEM)
    return pl.pallas_call(
        widen_kernel,
        in_specs=[vmem] * 3,
        out_specs=[vmem] * 2,
        out_shape=[
            jax.ShapeDtypeStruct((rows, cols, LANES), jnp.bfloat16),
            jax.ShapeDtypeStruct((rows, LANES, cols), jnp.bfloat16),
        ],
        compiler_params=pltpu.CompilerParams(vmem_limit_bytes=VMEM),
        cost_estimate=pl.CostEstimate(flops=10**10, bytes_accessed=10, transcendentals=0),
        name="widen_rows",
    )(other, wk, wv)


TILE_ROWS = ((0, 32), (32, 64), (0, 64), (64, 96), (96, 128), (64, 128))


def attend_kernel(begin, first, *refs):
    if first:
        k_other, v_other, *refs = refs
    else:
        _, other_ref, wk_ref, wv_ref, *refs = refs
    k_ref, v_ref, q_ref, g_ref, bias_ref, wo_ref, ob_ref, out_ref, v_both, *scratch = refs
    if not first:
        k_other, *scratch = scratch
    scores, weights, tops, shares = (scratch[2 * n : 2 * n + 2] for n in range(4))
    rows, cols, _ = k_other.shape
    keys = 2 * cols
    low = lax.broadcasted_iota(jnp.int32, (32, LANES), 1) < 64
    lanes = [slice(tile * LANES, (tile + 1) * LANES) for tile in range(6)]

    def blank(count):
        return jnp.zeros((count, LANES), jnp.bfloat16)

    def query_tile(row, tile):
        head, tail = TILE_ROWS[tile]
        if tile % 3 < 2:
            part = q_ref[begin + row, head:tail, :LANES]
        else:
            one = q_ref[begin + row, head : head + 32, LANES:]
            two = q_ref[begin + row, head + 32 : tail, LANES:]
            part = jnp.concatenate(
                (jnp.where(low, one, 0), jnp.where(low, 0, two)), 0
            ).astype(jnp.bfloat16)
        pieces = [part]
        if head:
            pieces.insert(0, blank(head))
        if tail < LANES:
            pieces.append(blank(LANES - tail))
        return jnp.concatenate(pieces, 0)

    def widen(row):
        if first:
            values = v_other[row]
        else:
            other = other_ref[row]
            k_other[row] = dot(other, wk_ref[...]).astype(jnp.bfloat16)
            yield
            values = dot(wv_ref[...], other, NT).astype(jnp.bfloat16)
        v_both[row] = jnp.concatenate((v_ref[begin + row], values), 1)
        yield

    def score(row, pair, slot, shift):
        for tile in range(3 * pair, 3 * pair + 3):
            query = query_tile(row, tile)
            both = jnp.concatenate((k_ref[begin + row], k_other[row]), 0)
            part = dot(both, query) + bias_ref[:keys, lanes[tile]]
            if shift:
                part = part + MISSING
            scores[slot][:, lanes[tile % 3]] = part
            tops[slot][0:1, lanes[tile % 3]] = jnp.max(part, axis=0, keepdims=True)
            yield

    def soften(slot):
        for tile in range(3):
            part = jnp.exp(scores[slot][:, lanes[tile]] - tops[slot][0:1, lanes[tile]])
            shares[slot][0:1, lanes[tile]] = 1.0 / jnp.sum(part, axis=0, keepdims=True)
            weights[slot][:, lanes[tile]] = part.astype(jnp.bfloat16)
            yield

    def mix(row, pair, slot, gated):
        mixed = []
        for tile in range(3):
            head, tail = TILE_ROWS[3 * pair + tile]
            part = dot(v_both[row, head:tail], weights[slot][:, lanes[tile]])
            mixed.append(part * shares[slot][0:1, lanes[tile]])
            yield
        one, two, both = mixed
        gate = g_ref[begin + row, 64 * pair : 64 * pair + 32]
        rest = jnp.where(low, both[:32] * gate[:, LANES:], 0.0)
        gated.append(jnp.concatenate((one * gate[:, :LANES], rest), 1))
        gate = g_ref[begin + row, 64 * pair + 32 : 64 * pair + 64]
        rest = jnp.where(low, 0.0, both[32:] * gate[:, LANES:])
        gated.append(jnp.concatenate((two * gate[:, :LANES], rest), 1))
        if pair:
            update = dot(jnp.concatenate(gated, 0).astype(jnp.bfloat16), wo_ref[...], TN)
            rest = cols - LANES
            update = jnp.concatenate(
                (update[:LANES], update[LANES : LANES + rest] + update[LANES + rest :]), 0
            )
            out_ref[row] = (update + ob_ref[...]).astype(jnp.bfloat16)
        yield

    def run(*stages):
        stages = list(stages)
        while stages:
            stages = [stage for stage in stages if next(stage, True) is None]

    present = bias_ref[keys, 0]

    @pl.when(present > 0.5)
    def _():
        run(widen(0))
        gated = [[] for _ in range(rows)]
        units = [(row, pair) for row in range(rows) for pair in range(2)]
        for step in range(len(units) + 2):
            stages = []
            if step >= 2:
                row, pair = units[step - 2]
                stages.append(mix(row, pair, step % 2, gated[row]))
            if 1 <= step <= len(units):
                stages.append(soften((step - 1) % 2))
            if step < len(units):
                stages.append(score(*units[step], step % 2, False))
                if units[step][1] == 0 and units[step][0] + 1 < rows:
                    stages.append(widen(units[step][0] + 1))
            run(*stages)

    @pl.when(present <= 0.5)
    def _():
        def one(row, carry):
            run(widen(row))
            gated = []
            for pair in range(2):
                run(score(row, pair, 0, True))
                run(soften(0))
                run(mix(row, pair, 0, gated))
            return carry

        lax.fori_loop(0, rows, one, 0)


def attend(head, k, v, q, g, bias, wo, ob, rows, begin):
    total, cols, _ = k.shape
    keys, lanes = 2 * cols, bias.shape[1]
    first = len(head) == 2
    vmem = pl.BlockSpec(memory_space=pltpu.VMEM)
    specs = [vmem] * 2 if first else [pl.BlockSpec(memory_space=pl.ANY)] + [vmem] * 3
    own_keys = [] if first else [pltpu.VMEM((rows, cols, LANES), jnp.bfloat16)]
    return pl.pallas_call(
        functools.partial(attend_kernel, begin, first),
        grid=(1,),
        in_specs=specs + [vmem] * 7,
        out_specs=pl.BlockSpec((rows, cols, LANES), lambda i: (begin // rows, 0, 0)),
        out_shape=jax.ShapeDtypeStruct((total, cols, LANES), jnp.bfloat16),
        scratch_shapes=[pltpu.VMEM((rows, LANES, keys), jnp.bfloat16)]
        + own_keys
        + [pltpu.VMEM((keys, lanes // 2), jnp.float32)] * 2
        + [pltpu.VMEM((keys, lanes // 2), jnp.bfloat16)] * 2
        + [pltpu.VMEM((8, lanes // 2), jnp.float32)] * 4,
        input_output_aliases={} if first else {0: 0},
        compiler_params=pltpu.CompilerParams(vmem_limit_bytes=24 << 20),
        cost_estimate=pl.CostEstimate(flops=10**10, bytes_accessed=10, transcendentals=0),
        name="attend_rows",
    )(*head, k, v, q, g, bias, wo, ob)


def device(z_hi, z_lo, y, core, x):
    return (((z_hi * 2 + z_lo) * 2 + y) * 2 + core) * 2 + x


def moved(array, move):
    pairs = []
    for number in range(32):
        a, b, y, c, x = ((number >> bit) & 1 for bit in (4, 3, 2, 1, 0))
        target = move(a, b, y, c, x)
        if target is not None:
            pairs.append((number, device(*target)))
    return lax.ppermute(array, ("rows", "cols"), pairs)


def spread_tiles(tile, z_hi, x, part):
    across = moved(tile, lambda a, b, y, c, x: None if a == x else (1 - a, b, y, c, 1 - x))
    straight = moved(tile, lambda a, b, y, c, x: (1 - a, b, y, c, x) if a == x else (a, b, y, c, 1 - x))
    across, part = lax.optimization_barrier((across, part))
    home = z_hi == x
    pair = jnp.stack((jnp.where(home, tile, straight), jnp.where(home, straight, across)))
    near = [pair]
    for move in (
        lambda a, b, y, c, x: (a, b, 1 - y, c, x),
        lambda a, b, y, c, x: (a, 1 - b, y, c, x),
        lambda a, b, y, c, x: (a, 1 - b, 1 - y, c, x),
    ):
        near.append(moved(pair, move))
    return jnp.concatenate(near, 0), part


def shards_general(
    pair, token_mask, norm_gain, norm_shift, in_weight, gate_bias, bias_weight, out_weight, out_bias
):
    row_count, col_count, channels = pair.shape
    head_count = bias_weight.shape[1]
    inner_width = out_weight.shape[0]
    head_size = inner_width // head_count
    normed = layer_norm(pair, norm_gain, norm_shift)
    flat_normed = normed.reshape(row_count * col_count, channels)
    bias_tile = jnp.einsum(
        "jkc,ch->jhk", normed, bias_weight, preferred_element_type=jnp.float32
    ).astype(jnp.bfloat16)
    bias_columns = lax.all_gather(bias_tile, "rows", axis=0, tiled=True)
    own_bias = lax.all_to_all(bias_columns, "cols", split_axis=0, concat_axis=2, tiled=True)
    query_gate = jnp.concatenate(
        (in_weight[:, :inner_width], in_weight[:, 3 * inner_width :]), axis=1
    )
    projected = jnp.dot(flat_normed, query_gate, preferred_element_type=jnp.float32)
    queries = (projected[:, :inner_width] * head_size ** (-0.5)).astype(jnp.bfloat16)
    queries = queries.reshape(row_count, col_count, head_count, head_size)
    gates = jax.nn.sigmoid(projected[:, inner_width:] + gate_bias)
    key_value_weight = in_weight[:, inner_width : 3 * inner_width]
    mask_row = token_mask.reshape(1, col_count)
    start_state = (
        jnp.full((row_count, col_count, head_count), -jnp.inf, jnp.float32),
        jnp.zeros((row_count, col_count, head_count), jnp.float32),
        jnp.zeros((row_count, col_count, inner_width), jnp.float32),
    )
    key_values = jnp.dot(flat_normed, key_value_weight, preferred_element_type=jnp.float32).astype(
        jnp.bfloat16
    )
    key_values = key_values.reshape(row_count, col_count, 2 * inner_width)
    pair_keys = lax.all_gather(key_values, "cols", axis=1, tiled=True)
    mask_in = lax.all_gather(mask_row, "cols", axis=1, tiled=True)
    state_now = start_state
    begin_at = jnp.int32(0)
    span_len = pair_keys.shape[1]
    for low_edge in range(0, span_len, col_count):
        high_edge = min(low_edge + col_count, span_len)
        attend_pair_keys = pair_keys[:, low_edge:high_edge]
        attend_begin_at = begin_at + low_edge
        attend_running_max, attend_totals, attend_summed = state_now
        attend_span_len = attend_pair_keys.shape[1]
        key_part = attend_pair_keys[..., :inner_width].reshape(
            row_count, attend_span_len, head_count, head_size
        )
        value_part = attend_pair_keys[..., inner_width:].reshape(
            row_count, attend_span_len, head_count, head_size
        )
        scores = jnp.einsum(
            "rjhd,rkhd->rjhk", queries, key_part, preferred_element_type=jnp.float32
        )
        bias_part = lax.dynamic_slice_in_dim(own_bias, attend_begin_at, attend_span_len, 2).astype(
            jnp.float32
        )
        masking = 1000000000.0 * (mask_in[:, low_edge:high_edge][0].astype(jnp.float32) - 1.0)
        scores = scores + bias_part + masking
        new_max = jnp.maximum(attend_running_max, jnp.max(scores, axis=-1))
        shrink = jnp.exp(attend_running_max - new_max)
        weights = jnp.exp(scores - new_max[..., None])
        attend_totals = attend_totals * shrink + jnp.sum(weights, axis=-1)
        mixed_part = jnp.einsum(
            "rjhk,rkhd->rjhd",
            weights.astype(jnp.bfloat16),
            value_part,
            preferred_element_type=jnp.float32,
        )
        attend_summed = (
            attend_summed.reshape(row_count, col_count, head_count, head_size) * shrink[..., None]
            + mixed_part
        )
        state_now = (
            new_max,
            attend_totals,
            attend_summed.reshape(row_count, col_count, inner_width),
        )
    running_max, totals, summed = state_now
    attended = summed.reshape(row_count, col_count, head_count, head_size) / totals[..., None]
    gated = gates.reshape(row_count, col_count, head_count, head_size) * attended
    gated = gated.astype(jnp.bfloat16).reshape(row_count * col_count, inner_width)
    updated = jnp.dot(gated, out_weight, preferred_element_type=jnp.float32) + out_bias
    return updated.astype(jnp.bfloat16).reshape(row_count, col_count, channels)


def fits(mesh, pair_shape, heads, inner):
    rows, cols, channels = pair_shape
    return (
        (mesh.shape["rows"], mesh.shape["cols"]) == (16, 2)
        and (rows, cols, channels) == (24, 192, LANES)
        and (heads, inner) == (4, LANES)
    )


def shards(
    pair, token_mask, norm_gain, norm_shift, in_weight, gate_bias, bias_weight, out_weight, out_bias
):
    rows, cols, channels = pair.shape
    inner = out_weight.shape[0]
    gain, shift = norm_gain.reshape(1, channels), norm_shift.reshape(1, channels)
    swap = [(0, 1), (1, 0)]
    *normed, tile = norm_and_tile(pair, gain, shift, bias_weight, token_mask, CHUNKS)
    wk, wv = in_weight[:, inner : 2 * inner], in_weight[:, 2 * inner : 3 * inner].T
    wqg = jnp.concatenate((in_weight[:, :inner].T, in_weight[:, 3 * inner :].T), 0)
    own = list(project(normed, (wk, wv, wqg, gate_bias.reshape(inner, 1))))
    row = lax.axis_index("rows")
    x = lax.axis_index("cols")
    z_hi, z_lo, y, core = row >> 3, (row >> 2) & 1, (row >> 1) & 1, row & 1
    near, normed[1] = spread_tiles(tile, z_hi, x, normed[1])
    near, *own = lax.optimization_barrier((near, *own))
    others = [lax.ppermute(part, "cols", swap) for part in normed[:2]]
    head = list(widen(others[0], wk, wv))
    normed[2], head[0] = lax.optimization_barrier((normed[2], head[0]))
    others.append(lax.ppermute(normed[2], "cols", swap))
    far = moved(near, lambda a, b, y, c, x: (a, b, y, 1 - c, x))
    place = jnp.arange(16, dtype=jnp.int32)
    half, a, b, c = place >> 3, (place >> 2) & 1, (place >> 1) & 1, place & 1
    index = (c ^ core) * 8 + (a ^ z_lo) * 4 + (b ^ y) * 2 + half
    bias = assemble(index, near, far, lane_order(cols, rows, 8))
    tail = (*own, bias, out_weight, out_bias.reshape(1, channels))
    out = attend(head, *tail, CHUNKS[0][1], CHUNKS[0][0])
    for (begin, count), other in zip(CHUNKS[1:], others[1:]):
        other, out = lax.optimization_barrier((other, out))
        out = attend((out, other, wk, wv), *tail, count, begin)
    return out


def solution(mesh):
    placed = (P("rows", "cols", None), P("cols"), P(), P(), P(), P(), P(), P(), P())

    def run(pair, *rest):
        tall, wide, channels = pair.shape
        block = (tall // mesh.shape["rows"], wide // mesh.shape["cols"], channels)
        bias_weight, out_weight = rest[5], rest[6]
        special = fits(mesh, block, bias_weight.shape[1], out_weight.shape[0])
        return jax.shard_map(
            shards if special else shards_general,
            mesh=mesh,
            in_specs=placed,
            out_specs=P("rows", "cols", None),
            check_vma=False,
        )(pair, *rest)

    return run
```

```python
import functools

import jax
import jax.numpy as jnp
import numpy as np
from jax import lax
from jax.experimental import pallas as pl
from jax.experimental.pallas import tpu as pltpu
from jax.sharding import PartitionSpec as P

LANES = 128
MISSING = -1e9
NN = (((1,), (0,)), ((), ()))
NT = (((1,), (1,)), ((), ()))
TN = (((0,), (0,)), ((), ()))
CHUNKS = ((0, 8), (8, 8), (16, 8))
VMEM = 14 << 20
ALL_VMEM = 60 << 20


def dot(left, right, dims=NN):
    return lax.dot_general(left, right, dims, preferred_element_type=jnp.float32)


def layer_norm(pair_block, norm_gain, norm_shift):
    as_float = pair_block.astype(jnp.float32)
    center = jnp.mean(as_float, axis=-1, keepdims=True)
    spread = jnp.mean(jnp.square(as_float - center), axis=-1, keepdims=True)
    return ((as_float - center) * lax.rsqrt(spread + 1e-05) * norm_gain + norm_shift).astype(
        jnp.bfloat16
    )


def normed_rows(block, mean_weight, gain, shift):
    center = block.astype(jnp.float32) - dot(block, mean_weight)
    spread = jnp.mean(center * center, axis=-1, keepdims=True)
    return (center * lax.rsqrt(spread + 1e-05) * gain + shift).astype(jnp.bfloat16)


def norm_kernel(parts, pair_hbm, *refs):
    small_hbm, refs = refs[:4], refs[4:]
    normed_refs, tile_ref, refs = refs[: len(parts)], refs[len(parts)], refs[len(parts) + 1 :]
    pair_ref, gain_ref, shift_ref, weight_ref, mask_ref, done = refs
    rows, slots = pair_ref.shape[0], 32
    copies = [
        pltpu.make_async_copy(source, target, done.at[place])
        for place, (source, target) in enumerate(
            zip(small_hbm, (gain_ref, shift_ref, weight_ref, mask_ref))
        )
    ]
    for place, (begin, count) in enumerate(parts):
        block = pl.ds(begin, count)
        copies.append(
            pltpu.make_async_copy(pair_hbm.at[block], pair_ref.at[block], done.at[4 + place])
        )
    for copy in copies:
        copy.start()
    for copy in copies[:4]:
        copy.wait()

    heads = weight_ref.shape[0]
    head = lax.broadcasted_iota(jnp.int32, (heads, LANES), 0)
    place = lax.broadcasted_iota(jnp.int32, (heads, LANES), 1)
    expand = jnp.logical_and(place >= head * slots, place < head * slots + slots)
    wide = dot(weight_ref[...], expand.astype(jnp.bfloat16), TN)
    spot = lax.broadcasted_iota(jnp.int32, (1, LANES), 1) == rows
    total = dot(mask_ref[...].astype(jnp.bfloat16), spot.astype(jnp.bfloat16), TN)
    slot = lax.rem(lax.broadcasted_iota(jnp.int32, (LANES, LANES), 1), slots)
    mean_weight = jnp.full((LANES, LANES), 1 / LANES, jnp.bfloat16)
    for (begin, count), copy, normed_ref in zip(parts, copies[4:], normed_refs):
        copy.wait()
        left, right = [], []
        for row in range(begin, begin + count):
            normed = normed_rows(pair_ref[row], mean_weight, gain_ref[...], shift_ref[...])
            normed_ref[row - begin] = normed
            left.append(normed)
            right.append(jnp.where(slot == row, wide, 0.0).astype(jnp.bfloat16))
        total += dot(jnp.concatenate(left, 1), jnp.concatenate(right, 0))
    tile_ref[...] = total.astype(jnp.bfloat16)


def norm_and_tile(pair, gain, shift, bias_weight, mask, parts):
    rows, cols, channels = pair.shape
    small = (gain, shift, bias_weight.T, mask.reshape(1, cols))
    vmem = pl.BlockSpec(memory_space=pltpu.VMEM)
    return pl.pallas_call(
        functools.partial(norm_kernel, parts),
        in_specs=[pl.BlockSpec(memory_space=pltpu.HBM)] * 5,
        out_specs=[vmem] * (len(parts) + 1),
        out_shape=[
            jax.ShapeDtypeStruct((count, cols, channels), jnp.bfloat16) for _, count in parts
        ]
        + [jax.ShapeDtypeStruct((cols, LANES), jnp.bfloat16)],
        scratch_shapes=[pltpu.VMEM(pair.shape, pair.dtype)]
        + [pltpu.VMEM(a.shape, a.dtype) for a in small]
        + [pltpu.SemaphoreType.DMA((4 + len(parts),))],
        compiler_params=pltpu.CompilerParams(vmem_limit_bytes=ALL_VMEM),
        cost_estimate=pl.CostEstimate(flops=10**9, bytes_accessed=10**7, transcendentals=0),
        name="norm_and_tile",
    )(pair, *small)


def assemble_kernel(index_ref, near_ref, far_ref, order_ref, bias_ref, tiles, marks):
    count, cols, _ = near_ref.shape
    tiles[:count] = near_ref[...]
    tiles[count:] = far_ref[...]
    for half in range(2):
        taken = [tiles[index_ref[half * count + place]] for place in range(count)]
        marks[half * cols : (half + 1) * cols] = taken[0].astype(jnp.float32)[:, 24:25]
        bias_ref[half * cols : (half + 1) * cols] = dot(
            jnp.concatenate(taken, 1), order_ref[...]
        )
    present = jnp.max(marks[...], axis=0, keepdims=True)
    hidden = jnp.logical_and(marks[...] < 0.5, present > 0.5)
    bias_ref[: 2 * cols] = jnp.where(hidden, MISSING, bias_ref[: 2 * cols])
    bias_ref[2 * cols :] = jnp.broadcast_to(present, (8, bias_ref.shape[1]))


def lane_order(cols, rows, places):
    order = np.zeros((places * LANES, 4 * cols), np.float32)
    for place in range(places):
        for head in range(4):
            for row in range(rows):
                query = place * rows + row
                base = (head // 2) * 2 * cols
                if query < LANES:
                    lane = base + (head % 2) * LANES + query
                else:
                    lane = base + 2 * LANES + (head % 2) * (cols - LANES) + query - LANES
                order[place * LANES + head * 32 + row, lane] = 1
    return jnp.asarray(order, jnp.bfloat16)


def assemble(index, near, far, order):
    count, cols, _ = near.shape
    vmem = pl.BlockSpec(memory_space=pltpu.VMEM)
    smem = pl.BlockSpec(memory_space=pltpu.SMEM)
    return pl.pallas_call(
        assemble_kernel,
        in_specs=[smem, vmem, vmem, vmem],
        out_specs=vmem,
        out_shape=jax.ShapeDtypeStruct((2 * cols + 8, order.shape[1]), jnp.float32),
        scratch_shapes=[
            pltpu.VMEM((2 * count, cols, LANES), jnp.bfloat16),
            pltpu.VMEM((2 * cols, 1), jnp.float32),
        ],
        compiler_params=pltpu.CompilerParams(vmem_limit_bytes=VMEM),
        cost_estimate=pl.CostEstimate(flops=10**9, bytes_accessed=4 * 10**6, transcendentals=0),
        name="assemble_bias",
    )(index, near, far, order)


def project_kernel(count, *refs):
    own_refs, refs = refs[:count], refs[count:]
    wk_ref, wv_ref, wqg_ref, gb_ref, k_ref, v_ref, q_ref, g_ref = refs
    begin = 0
    for own_ref in own_refs:
        rows, cols, channels = own_ref.shape
        keys = dot(own_ref[...].reshape(rows * cols, channels), wk_ref[...])
        k_ref[begin : begin + rows] = keys.astype(jnp.bfloat16).reshape(rows, cols, LANES)
        for row in range(rows):
            own = own_ref[row]
            v_ref[begin + row] = dot(wv_ref[...], own, NT).astype(jnp.bfloat16)
            mixed = dot(wqg_ref[...], jnp.concatenate((own, own[LANES:]), 0), NT)
            q_ref[begin + row] = (mixed[:LANES] * 32 ** (-0.5)).astype(jnp.bfloat16)
            g_ref[begin + row] = 0.5 * jnp.tanh(0.5 * (mixed[LANES:] + gb_ref[...])) + 0.5
        begin += rows


def project(parts, weights):
    cols, channels = parts[0].shape[1:]
    rows = sum(part.shape[0] for part in parts)
    vmem = pl.BlockSpec(memory_space=pltpu.VMEM)
    sizes = ((cols, LANES), (LANES, cols), (LANES, 2 * LANES), (LANES, 2 * LANES))
    kinds = (jnp.bfloat16,) * 3 + (jnp.float32,)
    return pl.pallas_call(
        functools.partial(project_kernel, len(parts)),
        in_specs=[vmem] * (len(parts) + len(weights)),
        out_specs=[vmem] * 4,
        out_shape=[jax.ShapeDtypeStruct((rows,) + size, kind) for size, kind in zip(sizes, kinds)],
        compiler_params=pltpu.CompilerParams(vmem_limit_bytes=VMEM),
        cost_estimate=pl.CostEstimate(flops=1, bytes_accessed=10, transcendentals=0),
        name="project_own",
    )(*parts, *weights)


def widen_kernel(other_ref, wk_ref, wv_ref, k_ref, v_ref):
    rows, cols, channels = other_ref.shape
    keys = dot(other_ref[...].reshape(rows * cols, channels), wk_ref[...])
    k_ref[...] = keys.astype(jnp.bfloat16).reshape(rows, cols, LANES)
    for row in range(rows):
        v_ref[row] = dot(wv_ref[...], other_ref[row], NT).astype(jnp.bfloat16)


def widen(other, wk, wv):
    rows, cols, _ = other.shape
    vmem = pl.BlockSpec(memory_space=pltpu.VMEM)
    return pl.pallas_call(
        widen_kernel,
        in_specs=[vmem] * 3,
        out_specs=[vmem] * 2,
        out_shape=[
            jax.ShapeDtypeStruct((rows, cols, LANES), jnp.bfloat16),
            jax.ShapeDtypeStruct((rows, LANES, cols), jnp.bfloat16),
        ],
        compiler_params=pltpu.CompilerParams(vmem_limit_bytes=VMEM),
        cost_estimate=pl.CostEstimate(flops=10**10, bytes_accessed=10, transcendentals=0),
        name="widen_rows",
    )(other, wk, wv)


TILE_ROWS = ((0, 32), (32, 64), (0, 64), (64, 96), (96, 128), (64, 128))


def attend_kernel(begin, first, *refs):
    if first:
        k_other, v_other, *refs = refs
    else:
        _, other_ref, wk_ref, wv_ref, *refs = refs
    k_ref, v_ref, q_ref, g_ref, bias_ref, wo_ref, ob_ref, out_ref, v_both, *scratch = refs
    if not first:
        k_other, *scratch = scratch
    scores, weights, tops, shares = (scratch[2 * n : 2 * n + 2] for n in range(4))
    rows, cols, _ = k_other.shape
    keys = 2 * cols
    low = lax.broadcasted_iota(jnp.int32, (32, LANES), 1) < 64
    lanes = [slice(tile * LANES, (tile + 1) * LANES) for tile in range(6)]

    def blank(count):
        return jnp.zeros((count, LANES), jnp.bfloat16)

    def query_tile(row, tile):
        head, tail = TILE_ROWS[tile]
        if tile % 3 < 2:
            part = q_ref[begin + row, head:tail, :LANES]
        else:
            one = q_ref[begin + row, head : head + 32, LANES:]
            two = q_ref[begin + row, head + 32 : tail, LANES:]
            part = jnp.concatenate(
                (jnp.where(low, one, 0), jnp.where(low, 0, two)), 0
            ).astype(jnp.bfloat16)
        pieces = [part]
        if head:
            pieces.insert(0, blank(head))
        if tail < LANES:
            pieces.append(blank(LANES - tail))
        return jnp.concatenate(pieces, 0)

    def widen(row):
        if first:
            values = v_other[row]
        else:
            other = other_ref[row]
            k_other[row] = dot(other, wk_ref[...]).astype(jnp.bfloat16)
            yield
            values = dot(wv_ref[...], other, NT).astype(jnp.bfloat16)
        v_both[row] = jnp.concatenate((v_ref[begin + row], values), 1)
        yield

    def score(row, pair, slot, shift):
        for tile in range(3 * pair, 3 * pair + 3):
            query = query_tile(row, tile)
            both = jnp.concatenate((k_ref[begin + row], k_other[row]), 0)
            part = dot(both, query) + bias_ref[:keys, lanes[tile]]
            if shift:
                part = part + MISSING
            scores[slot][:, lanes[tile % 3]] = part
            tops[slot][0:1, lanes[tile % 3]] = jnp.max(part, axis=0, keepdims=True)
            yield

    def soften(slot):
        for tile in range(3):
            part = jnp.exp(scores[slot][:, lanes[tile]] - tops[slot][0:1, lanes[tile]])
            shares[slot][0:1, lanes[tile]] = 1.0 / jnp.sum(part, axis=0, keepdims=True)
            weights[slot][:, lanes[tile]] = part.astype(jnp.bfloat16)
            yield

    def mix(row, pair, slot, gated):
        mixed = []
        for tile in range(3):
            head, tail = TILE_ROWS[3 * pair + tile]
            part = dot(v_both[row, head:tail], weights[slot][:, lanes[tile]])
            mixed.append(part * shares[slot][0:1, lanes[tile]])
            yield
        one, two, both = mixed
        gate = g_ref[begin + row, 64 * pair : 64 * pair + 32]
        rest = jnp.where(low, both[:32] * gate[:, LANES:], 0.0)
        gated.append(jnp.concatenate((one * gate[:, :LANES], rest), 1))
        gate = g_ref[begin + row, 64 * pair + 32 : 64 * pair + 64]
        rest = jnp.where(low, 0.0, both[32:] * gate[:, LANES:])
        gated.append(jnp.concatenate((two * gate[:, :LANES], rest), 1))
        if pair:
            update = dot(jnp.concatenate(gated, 0).astype(jnp.bfloat16), wo_ref[...], TN)
            rest = cols - LANES
            update = jnp.concatenate(
                (update[:LANES], update[LANES : LANES + rest] + update[LANES + rest :]), 0
            )
            out_ref[row] = (update + ob_ref[...]).astype(jnp.bfloat16)
        yield

    def run(*stages):
        stages = list(stages)
        while stages:
            stages = [stage for stage in stages if next(stage, True) is None]

    present = bias_ref[keys, 0]

    @pl.when(present > 0.5)
    def _():
        run(widen(0))
        gated = [[] for _ in range(rows)]
        units = [(row, pair) for row in range(rows) for pair in range(2)]
        for step in range(len(units) + 2):
            stages = []
            if step >= 2:
                row, pair = units[step - 2]
                stages.append(mix(row, pair, step % 2, gated[row]))
            if 1 <= step <= len(units):
                stages.append(soften((step - 1) % 2))
            if step < len(units):
                stages.append(score(*units[step], step % 2, False))
                if units[step][1] == 0 and units[step][0] + 1 < rows:
                    stages.append(widen(units[step][0] + 1))
            stages = stages[::-1]
            run(*stages)

    @pl.when(present <= 0.5)
    def _():
        def one(row, carry):
            run(widen(row))
            gated = []
            for pair in range(2):
                run(score(row, pair, 0, True))
                run(soften(0))
                run(mix(row, pair, 0, gated))
            return carry

        lax.fori_loop(0, rows, one, 0)


def attend(head, k, v, q, g, bias, wo, ob, rows, begin):
    total, cols, _ = k.shape
    keys, lanes = 2 * cols, bias.shape[1]
    first = len(head) == 2
    vmem = pl.BlockSpec(memory_space=pltpu.VMEM)
    specs = [vmem] * 2 if first else [pl.BlockSpec(memory_space=pl.ANY)] + [vmem] * 3
    own_keys = [] if first else [pltpu.VMEM((rows, cols, LANES), jnp.bfloat16)]
    return pl.pallas_call(
        functools.partial(attend_kernel, begin, first),
        grid=(1,),
        in_specs=specs + [vmem] * 7,
        out_specs=pl.BlockSpec((rows, cols, LANES), lambda i: (begin // rows, 0, 0)),
        out_shape=jax.ShapeDtypeStruct((total, cols, LANES), jnp.bfloat16),
        scratch_shapes=[pltpu.VMEM((rows, LANES, keys), jnp.bfloat16)]
        + own_keys
        + [pltpu.VMEM((keys, lanes // 2), jnp.float32)] * 2
        + [pltpu.VMEM((keys, lanes // 2), jnp.bfloat16)] * 2
        + [pltpu.VMEM((8, lanes // 2), jnp.float32)] * 4,
        input_output_aliases={} if first else {0: 0},
        compiler_params=pltpu.CompilerParams(vmem_limit_bytes=24 << 20),
        cost_estimate=pl.CostEstimate(flops=10**10, bytes_accessed=10, transcendentals=0),
        name="attend_rows",
    )(*head, k, v, q, g, bias, wo, ob)


def device(z_hi, z_lo, y, core, x):
    return (((z_hi * 2 + z_lo) * 2 + y) * 2 + core) * 2 + x


def moved(array, move):
    pairs = []
    for number in range(32):
        a, b, y, c, x = ((number >> bit) & 1 for bit in (4, 3, 2, 1, 0))
        target = move(a, b, y, c, x)
        if target is not None:
            pairs.append((number, device(*target)))
    return lax.ppermute(array, ("rows", "cols"), pairs)


def spread_tiles(tile, z_hi, x, part):
    across = moved(tile, lambda a, b, y, c, x: None if a == x else (1 - a, b, y, c, 1 - x))
    straight = moved(tile, lambda a, b, y, c, x: (1 - a, b, y, c, x) if a == x else (a, b, y, c, 1 - x))
    across, part = lax.optimization_barrier((across, part))
    home = z_hi == x
    pair = jnp.stack((jnp.where(home, tile, straight), jnp.where(home, straight, across)))
    near = [pair]
    for move in (
        lambda a, b, y, c, x: (a, b, 1 - y, c, x),
        lambda a, b, y, c, x: (a, 1 - b, y, c, x),
        lambda a, b, y, c, x: (a, 1 - b, 1 - y, c, x),
    ):
        near.append(moved(pair, move))
    return jnp.concatenate(near, 0), part


def shards_general(
    pair, token_mask, norm_gain, norm_shift, in_weight, gate_bias, bias_weight, out_weight, out_bias
):
    row_count, col_count, channels = pair.shape
    head_count = bias_weight.shape[1]
    inner_width = out_weight.shape[0]
    head_size = inner_width // head_count
    normed = layer_norm(pair, norm_gain, norm_shift)
    flat_normed = normed.reshape(row_count * col_count, channels)
    bias_tile = jnp.einsum(
        "jkc,ch->jhk", normed, bias_weight, preferred_element_type=jnp.float32
    ).astype(jnp.bfloat16)
    bias_columns = lax.all_gather(bias_tile, "rows", axis=0, tiled=True)
    own_bias = lax.all_to_all(bias_columns, "cols", split_axis=0, concat_axis=2, tiled=True)
    query_gate = jnp.concatenate(
        (in_weight[:, :inner_width], in_weight[:, 3 * inner_width :]), axis=1
    )
    projected = jnp.dot(flat_normed, query_gate, preferred_element_type=jnp.float32)
    queries = (projected[:, :inner_width] * head_size ** (-0.5)).astype(jnp.bfloat16)
    queries = queries.reshape(row_count, col_count, head_count, head_size)
    gates = jax.nn.sigmoid(projected[:, inner_width:] + gate_bias)
    key_value_weight = in_weight[:, inner_width : 3 * inner_width]
    mask_row = token_mask.reshape(1, col_count)
    start_state = (
        jnp.full((row_count, col_count, head_count), -jnp.inf, jnp.float32),
        jnp.zeros((row_count, col_count, head_count), jnp.float32),
        jnp.zeros((row_count, col_count, inner_width), jnp.float32),
    )
    key_values = jnp.dot(flat_normed, key_value_weight, preferred_element_type=jnp.float32).astype(
        jnp.bfloat16
    )
    key_values = key_values.reshape(row_count, col_count, 2 * inner_width)
    pair_keys = lax.all_gather(key_values, "cols", axis=1, tiled=True)
    mask_in = lax.all_gather(mask_row, "cols", axis=1, tiled=True)
    state_now = start_state
    begin_at = jnp.int32(0)
    span_len = pair_keys.shape[1]
    for low_edge in range(0, span_len, col_count):
        high_edge = min(low_edge + col_count, span_len)
        attend_pair_keys = pair_keys[:, low_edge:high_edge]
        attend_begin_at = begin_at + low_edge
        attend_running_max, attend_totals, attend_summed = state_now
        attend_span_len = attend_pair_keys.shape[1]
        key_part = attend_pair_keys[..., :inner_width].reshape(
            row_count, attend_span_len, head_count, head_size
        )
        value_part = attend_pair_keys[..., inner_width:].reshape(
            row_count, attend_span_len, head_count, head_size
        )
        scores = jnp.einsum(
            "rjhd,rkhd->rjhk", queries, key_part, preferred_element_type=jnp.float32
        )
        bias_part = lax.dynamic_slice_in_dim(own_bias, attend_begin_at, attend_span_len, 2).astype(
            jnp.float32
        )
        masking = 1000000000.0 * (mask_in[:, low_edge:high_edge][0].astype(jnp.float32) - 1.0)
        scores = scores + bias_part + masking
        new_max = jnp.maximum(attend_running_max, jnp.max(scores, axis=-1))
        shrink = jnp.exp(attend_running_max - new_max)
        weights = jnp.exp(scores - new_max[..., None])
        attend_totals = attend_totals * shrink + jnp.sum(weights, axis=-1)
        mixed_part = jnp.einsum(
            "rjhk,rkhd->rjhd",
            weights.astype(jnp.bfloat16),
            value_part,
            preferred_element_type=jnp.float32,
        )
        attend_summed = (
            attend_summed.reshape(row_count, col_count, head_count, head_size) * shrink[..., None]
            + mixed_part
        )
        state_now = (
            new_max,
            attend_totals,
            attend_summed.reshape(row_count, col_count, inner_width),
        )
    running_max, totals, summed = state_now
    attended = summed.reshape(row_count, col_count, head_count, head_size) / totals[..., None]
    gated = gates.reshape(row_count, col_count, head_count, head_size) * attended
    gated = gated.astype(jnp.bfloat16).reshape(row_count * col_count, inner_width)
    updated = jnp.dot(gated, out_weight, preferred_element_type=jnp.float32) + out_bias
    return updated.astype(jnp.bfloat16).reshape(row_count, col_count, channels)


def fits(mesh, pair_shape, heads, inner):
    rows, cols, channels = pair_shape
    return (
        (mesh.shape["rows"], mesh.shape["cols"]) == (16, 2)
        and (rows, cols, channels) == (24, 192, LANES)
        and (heads, inner) == (4, LANES)
    )


def shards(
    pair, token_mask, norm_gain, norm_shift, in_weight, gate_bias, bias_weight, out_weight, out_bias
):
    rows, cols, channels = pair.shape
    inner = out_weight.shape[0]
    gain, shift = norm_gain.reshape(1, channels), norm_shift.reshape(1, channels)
    swap = [(0, 1), (1, 0)]
    *normed, tile = norm_and_tile(pair, gain, shift, bias_weight, token_mask, CHUNKS)
    wk, wv = in_weight[:, inner : 2 * inner], in_weight[:, 2 * inner : 3 * inner].T
    wqg = jnp.concatenate((in_weight[:, :inner].T, in_weight[:, 3 * inner :].T), 0)
    own = list(project(normed, (wk, wv, wqg, gate_bias.reshape(inner, 1))))
    row = lax.axis_index("rows")
    x = lax.axis_index("cols")
    z_hi, z_lo, y, core = row >> 3, (row >> 2) & 1, (row >> 1) & 1, row & 1
    near, normed[1] = spread_tiles(tile, z_hi, x, normed[1])
    near, *own = lax.optimization_barrier((near, *own))
    others = [lax.ppermute(part, "cols", swap) for part in normed[:2]]
    head = list(widen(others[0], wk, wv))
    normed[2], head[0] = lax.optimization_barrier((normed[2], head[0]))
    others.append(lax.ppermute(normed[2], "cols", swap))
    far = moved(near, lambda a, b, y, c, x: (a, b, y, 1 - c, x))
    place = jnp.arange(16, dtype=jnp.int32)
    half, a, b, c = place >> 3, (place >> 2) & 1, (place >> 1) & 1, place & 1
    index = (c ^ core) * 8 + (a ^ z_lo) * 4 + (b ^ y) * 2 + half
    bias = assemble(index, near, far, lane_order(cols, rows, 8))
    tail = (*own, bias, out_weight, out_bias.reshape(1, channels))
    out = attend(head, *tail, CHUNKS[0][1], CHUNKS[0][0])
    for (begin, count), other in zip(CHUNKS[1:], others[1:]):
        other, out = lax.optimization_barrier((other, out))
        out = attend((out, other, wk, wv), *tail, count, begin)
    return out


def solution(mesh):
    placed = (P("rows", "cols", None), P("cols"), P(), P(), P(), P(), P(), P(), P())

    def run(pair, *rest):
        tall, wide, channels = pair.shape
        block = (tall // mesh.shape["rows"], wide // mesh.shape["cols"], channels)
        bias_weight, out_weight = rest[5], rest[6]
        special = fits(mesh, block, bias_weight.shape[1], out_weight.shape[0])
        return jax.shard_map(
            shards if special else shards_general,
            mesh=mesh,
            in_specs=placed,
            out_specs=P("rows", "cols", None),
            check_vma=False,
        )(pair, *rest)

    return run
```
